32 devices in a mesh: row: 8 (over y, x, core), col: 4 (over z).
Axes of the slice: x: 2, y: 2, z: 4, core: 2. Of those that a mesh axis runs over, the one named last changes fastest.
Arguments:
- images: bfloat16 [8, 32, 128, 256], P('row', 'col'), may hold values from -6 to 6
- weight: bfloat16 [3, 3, 256, 256], P(None, None, None, 'col'), may hold values from -0.125 to 0.125
- norm_gain: float32 [256], replicated, may hold values from 0.5 to 1.5
- cotangent: bfloat16 [8, 32, 128, 256], P('row', 'col'), may hold values from -6 to 6
Outputs:
- features: bfloat16 [8, 32, 128, 256], P('row', 'col')
- input_grad: bfloat16 [8, 32, 128, 256], P('row', 'col')
- weight_grad: float32 [3, 3, 256, 256], P(None, None, None, 'col')
The draws below stay inside these ranges and needn't reach their ends.
All inputs are finite; a program needn't handle non-finite values.
Results may differ from the reference program's by a relative error of at most 0.013.
Values may be sent and summed in bfloat16 or wider, within the bound.
A program may use at most 64 MiB of HBM per device.

```python
import math
import jax
import jax.numpy as jnp
from jax import lax

CIN = 256
COUT = 256
W = 128
IMGS = 8
H = 32
PIXELS = 32768


def raised(array, own_key, source, target, parts, factor):
    def block_of(axis_at):
        return (jnp.arange(array.shape[axis_at]) // (array.shape[axis_at] // parts)).reshape((-1,) + (1,) * (array.ndim - 1 - axis_at))

    first = jax.random.permutation(own_key, parts)[block_of(target)]
    far = (block_of(target) + parts // 2) % parts
    return jnp.where((block_of(source) == first) | (block_of(source) == far), factor * array, array)


def level_of(stream_key, shape, cuts, least, high):
    loudness = 1.0
    for position, parts in cuts:
        steps = jax.random.uniform(jax.random.fold_in(jax.random.fold_in(stream_key, 6), position), (parts,), jnp.float32, least / len(cuts), high / len(cuts))
        loudness = loudness * jnp.repeat(jnp.exp(steps), shape[position] // parts).reshape((-1,) + (1,) * (len(shape) - 1 - position))
    return loudness


def scatter_about(key, dims, deviation, reach, cuts=(), held_as=jnp.bfloat16):
    values = jax.random.normal(key, dims, jnp.float32) * deviation
    if len(cuts) > 0:
        values = level_of(key, dims, cuts, -0.22, 0.18) * values
    return jnp.clip(values, min=-reach, max=reach).astype(held_as)


def noise_with(stream_key, extent, scale, limit, cuts, heavy, dtype=jnp.bfloat16):
    array = scale * jax.random.normal(stream_key, extent, jnp.float32)
    if cuts:
        array = array * level_of(stream_key, extent, cuts, -0.22, 0.18)
    return jnp.clip(raised(array, jax.random.fold_in(stream_key, 3), *heavy), -limit, limit).astype(dtype)


def setup_inputs(seed: int = 0) -> dict:
    key_list = jax.random.split(jax.random.key(seed), 5)
    return {
        "images": scatter_about(key_list[0], (IMGS, H, W, CIN), 1.0, 6.0, ((0, 8), (1, 4))),
        "weight": scatter_about(key_list[1], (3, 3, CIN, COUT), (9 * CIN) ** -0.5, 0.125, ((3, 4),)),
        "norm_gain": jnp.clip(1.0 + 0.1 * jax.random.normal(key_list[2], (COUT,), jnp.float32), 0.5, 1.5),
        "cotangent": noise_with(key_list[3], (IMGS, H, W, COUT), 1.0, 6.0, ((0, 8), (1, 4)), (1, 3, 4, 2.0)),
    }


epsilon = 1e-06
root_half = 0.7071067811865476
norm_const = 0.3989422804014327

def norm_act(conv_out, upper, norm_gain):
    mean_val = lax.optimization_barrier(jnp.mean(conv_out, axis=-1, keepdims=True))
    centred = conv_out - mean_val
    variance = lax.optimization_barrier(jnp.mean(centred * centred, axis=-1, keepdims=True))
    inv_std = lax.rsqrt(variance + epsilon)
    unit = centred * inv_std
    normed = unit * norm_gain
    cdf_val = 0.5 * (1.0 + lax.erf(normed * root_half))
    density = jnp.exp(-0.5 * normed * normed) * norm_const
    outputs = (normed * cdf_val).astype(jnp.bfloat16)
    upstream = upper.astype(jnp.float32) * (cdf_val + normed * density) * norm_gain
    mean_up = lax.optimization_barrier(jnp.mean(upstream, axis=-1, keepdims=True))
    mean_cross = lax.optimization_barrier(jnp.mean(upstream * unit, axis=-1, keepdims=True))
    grad_pre = inv_std * (upstream - mean_up - unit * mean_cross)
    return (outputs, grad_pre.astype(jnp.bfloat16))

def window(padded, tap_row, tap_col):
    return padded[tap_row:tap_row + H, tap_col:tap_col + W, :].reshape(H * W, padded.shape[-1])

def reference(images, weight, norm_gain, cotangent):

    def one_image(running, sample):
        image_one, cot_one = sample
        padded = jnp.pad(image_one, ((1, 1), (1, 1), (0, 0)))
        conv_out = jnp.zeros((H * W, COUT), jnp.float32)
        for tap_row in range(3):
            for tap_col in range(3):
                conv_out = conv_out + jnp.dot(window(padded, tap_row, tap_col), weight[tap_row, tap_col], preferred_element_type=jnp.float32)
        outputs, grad_pre = norm_act(conv_out, cot_one.reshape(H * W, COUT), norm_gain)
        grad_pad = jnp.pad(grad_pre.reshape(H, W, COUT), ((1, 1), (1, 1), (0, 0)))
        grad_input = jnp.zeros((H * W, CIN), jnp.float32)
        pieces = []
        for tap_row in range(3):
            for tap_col in range(3):
                grad_input = grad_input + lax.dot_general(window(grad_pad, 2 - tap_row, 2 - tap_col), weight[tap_row, tap_col], (((1,), (1,)), ((), ())), preferred_element_type=jnp.float32)
                pieces.append(lax.dot_general(window(padded, tap_row, tap_col), grad_pre, (((0,), (0,)), ((), ())), preferred_element_type=jnp.float32))
        stacked = jnp.stack(pieces).reshape(3, 3, CIN, COUT)
        return (running + stacked, (outputs.reshape(H, W, COUT), grad_input.astype(jnp.bfloat16).reshape(H, W, CIN)))
    running, results = lax.scan(one_image, jnp.zeros((3, 3, CIN, COUT), jnp.float32), (images, cotangent))
    features, input_grad = results
    weight_grad = running * (1.0 / math.sqrt(PIXELS))
    return (features, input_grad, weight_grad)
```

```python
import functools
import math

import jax
import jax.numpy as jnp
from jax import lax
from jax.experimental import pallas as pl
from jax.experimental.pallas import tpu as pltpu
from jax.sharding import PartitionSpec as P

epsilon = 1e-06
root_half = 0.7071067811865476
norm_const = 0.3989422804014327
MESH = pl.DeviceIdType.MESH
NT = (((1,), (1,)), ((), ()))


def norm_act(conv_out, upper, norm_gain):
    mean_val = jnp.mean(conv_out, axis=-1, keepdims=True)
    centred = conv_out - mean_val
    variance = jnp.mean(centred * centred, axis=-1, keepdims=True)
    inv_std = lax.rsqrt(variance + epsilon)
    unit = centred * inv_std
    normed = unit * norm_gain
    cdf_val = 0.5 * (1.0 + lax.erf(normed * root_half))
    density = jnp.exp(-0.5 * normed * normed) * norm_const
    outputs = (normed * cdf_val).astype(jnp.bfloat16)
    upstream = upper.astype(jnp.float32) * (cdf_val + normed * density) * norm_gain
    mean_up = jnp.mean(upstream, axis=-1, keepdims=True)
    mean_cross = jnp.mean(upstream * unit, axis=-1, keepdims=True)
    return (outputs, inv_std * (upstream - mean_up - unit * mean_cross))


def kernel(
    plan,
    x_ref,
    w_ref,
    gain_ref,
    cot_ref,
    feat_ref,
    igrad_ref,
    wg_ref,
    wt,
    x3,
    g3,
    gt,
    conv,
    x_halo,
    g_halo,
    parts,
    parts_in,
    gathered,
    z_in,
    *rest,
):
    rows, cols, quads, split, cs, rs = plan
    phases = quads.bit_length() - 1
    totals, totals_in = rest[: phases + 1], rest[phases + 1 : 2 * phases + 1]
    (halo_s, halo_r, wz_s, wz_r, wq_s, wq_r, sib_s, sib_r, ph_s, ph_r, z_s, z_r, ag_s, ag_r) = rest[
        2 * phases + 1 :
    ]
    tile_rows, width, chan = x_ref.shape
    out_chan = cs * cols
    taps = 3 * chan
    half_k = taps // 2
    half_w = 3 * half_k
    my_row, my_col = lax.axis_index("row"), lax.axis_index("col")
    quad, core = my_row // 2, my_row % 2
    sibling = (quad * 2 + 1 - core, my_col)
    bits, partners, partner_quads = [], [], []
    for j in range(phases):
        low, high = 1 << j, 1 << (phases - 1 - j)
        mask = low + core * (high - low)
        bit = (1 - core) * ((quad // low) % 2) + core * ((quad // high) % 2)
        other = quad + mask * (1 - 2 * bit)
        bits.append(bit)
        partner_quads.append(other)
        partners.append((other * 2 + core, my_col))
    started = []

    def send(src, dst, send_sem, recv_sem, device):
        copy = pltpu.make_async_remote_copy(
            src_ref=src,
            dst_ref=dst,
            send_sem=send_sem,
            recv_sem=recv_sem,
            device_id=device,
            device_id_type=MESH,
        )
        copy.start()
        started.append(copy)
        return copy

    def col_at(shift):
        return (my_col + cols + shift) % cols

    barrier = pltpu.get_barrier_semaphore()
    for d in range(1, rows):
        pl.semaphore_signal(
            barrier, inc=1, device_id=((my_row + d) % rows, my_col), device_id_type=MESH
        )
    for d in range(1, cols):
        pl.semaphore_signal(barrier, inc=1, device_id=(my_row, col_at(d)), device_id_type=MESH)

    eye = (
        lax.broadcasted_iota(jnp.int32, (cs, cs), 0) == lax.broadcasted_iota(jnp.int32, (cs, cs), 1)
    ).astype(jnp.bfloat16)
    own_rows = pl.ds(pl.multiple_of(my_col * cs, 16), cs)
    for k in range(3):
        wt[own_rows, k * taps : (k + 1) * taps] = lax.dot_general(
            eye, w_ref[k * taps : (k + 1) * taps, :], NT, preferred_element_type=jnp.float32
        ).astype(jnp.bfloat16)

    pl.semaphore_wait(barrier, rows + cols - 2)

    half_lanes = pl.ds(pl.multiple_of(core * half_w, 128), half_w)

    def piece(col, q):
        start = col * cs + (q * rs if split else 0)
        return wt.at[pl.ds(pl.multiple_of(start, 16), rs), half_lanes]

    wz = [None]
    for d in range(1, cols):
        own = piece(my_col, quad)
        wz.append(send(own, own, wz_s.at[d - 1], wz_r.at[d - 1], (my_row, col_at(d))))

    has_up, has_down = my_col > 0, my_col < cols - 1

    def halo_copies(first, last, into, base):
        up = pltpu.make_async_remote_copy(
            src_ref=first,
            dst_ref=into.at[1],
            send_sem=halo_s.at[base],
            recv_sem=halo_r.at[base],
            device_id=(my_row, col_at(-1)),
            device_id_type=MESH,
        )
        down = pltpu.make_async_remote_copy(
            src_ref=last,
            dst_ref=into.at[0],
            send_sem=halo_s.at[base + 1],
            recv_sem=halo_r.at[base + 1],
            device_id=(my_row, col_at(1)),
            device_id_type=MESH,
        )

        @pl.when(has_up)
        def _():
            up.start()

        @pl.when(has_down)
        def _():
            down.start()

        return up, down

    column = lax.broadcasted_iota(jnp.int32, (width, chan), 0)

    def spread(dst, row, value, flip):
        value = value.astype(jnp.float32)
        left = jnp.where(column == 0, 0.0, pltpu.roll(value, 1, 0))
        right = jnp.where(column == width - 1, 0.0, pltpu.roll(value, width - 1, 0))
        shifted = (right, value, left) if flip else (left, value, right)
        for c in range(3):
            dst[row, :, c * chan : (c + 1) * chan] = shifted[c].astype(jnp.bfloat16)

    def halo_rows(dst, into, copies, flip):
        up, down = copies

        @pl.when(has_up)
        def _():
            down.wait_recv()
            spread(dst, 0, into[0], flip)

        @pl.when(jnp.logical_not(has_up))
        def _():
            dst[0] = jnp.zeros(dst.shape[1:], dst.dtype)

        @pl.when(has_down)
        def _():
            up.wait_recv()
            spread(dst, tile_rows + 1, into[1], flip)

        @pl.when(jnp.logical_not(has_down))
        def _():
            dst[tile_rows + 1] = jnp.zeros(dst.shape[1:], dst.dtype)

    x_copies = halo_copies(x_ref.at[0], x_ref.at[tile_rows - 1], x_halo, 0)

    hops = {}
    if split:
        for d in range(1, cols):
            wz[d].wait_recv()
            got = piece(col_at(-d), quad)
            for j in range(2):
                hops[d, j] = send(got, got, wq_s.at[d - 1, j], wq_r.at[d - 1, j], partners[j])

    @pl.loop(0, tile_rows)
    def _(i):
        spread(x3, i + 1, x_ref[i], False)

    if split:
        for d in range(1, cols):
            hops[d, 0].wait_recv()
            got = piece(col_at(-d), partner_quads[0])
            hops[d, 2] = send(got, got, wq_s.at[d - 1, 2], wq_r.at[d - 1, 2], partners[1])
    halo_rows(x3, x_halo, x_copies, False)
    sib = []
    for d in range(1, cols):
        if split:
            hops[d, 1].wait_recv()
            hops[d, 2].wait_recv()
        else:
            wz[d].wait_recv()
        block = wt.at[pl.ds(pl.multiple_of(col_at(-d) * cs, 16), cs), half_lanes]
        sib.append(send(block, block, sib_s.at[d - 1], sib_r.at[d - 1], sibling))
    for copy in sib:
        copy.wait_recv()

    gain = gain_ref[...]
    half_rows = tile_rows // 2
    for b in range(2):
        acc = None
        for a in range(3):
            term = lax.dot_general(
                x3[b * half_rows + a : (b + 1) * half_rows + a].reshape(half_rows * width, taps),
                wt[:, a * taps : (a + 1) * taps],
                NT,
                preferred_element_type=jnp.float32,
            )
            acc = term if acc is None else acc + term
        conv[b * half_rows : (b + 1) * half_rows] = acc.reshape(half_rows, width, out_chan)

    @pl.loop(0, tile_rows)
    def _(i):
        outputs, grad_pre = norm_act(conv[i], cot_ref[i], gain)
        feat_ref[i] = outputs
        spread(g3, i + 1, grad_pre, True)
        gt[:, pl.ds(pl.multiple_of(i * width, 128), width)] = grad_pre.T.astype(jnp.bfloat16)

    centre = pl.ds(chan, chan)
    g_copies = halo_copies(g3.at[1, :, centre], g3.at[tile_rows, :, centre], g_halo, 2)

    def weight_part(k):
        acc = jnp.dot(
            gt[...],
            x3[k : k + tile_rows].reshape(tile_rows * width, taps),
            preferred_element_type=jnp.float32,
        ).astype(jnp.bfloat16)
        for h in range(2):
            for s in range(quads if split else 1):
                at = (s % 2) * 2 + s // 2 if split and h == 0 else s
                for c in range(cols):
                    first = c * cs + s * rs
                    parts[k, h, at, c] = acc[first : first + rs, h * half_k : (h + 1) * half_k]
        return send(
            parts.at[k, 1 - core], parts_in.at[k], ph_s.at[k, phases], ph_r.at[k, phases], sibling
        )

    def add(one, two):
        return (one.astype(jnp.float32) + two.astype(jnp.float32)).astype(jnp.bfloat16)

    def start_phase(k, j):
        size = totals_in[j].shape[1]
        source = totals[j].at[k, pl.ds((1 - bits[j]) * size, size)] if split else totals[j].at[k]
        return send(source, totals_in[j].at[k], ph_s.at[k, j], ph_r.at[k, j], partners[j])

    def after_siblings(k, copy):
        copy.wait_recv()
        totals[0][k] = add(parts[k, core], parts_in[k])
        return start_phase(k, 0)

    def after_phase(k, j, copy):
        copy.wait_recv()
        size = totals_in[j].shape[1]
        kept = totals[j][k, pl.ds(bits[j] * size, size)] if split else totals[j][k]
        totals[j + 1][k] = add(kept, totals_in[j][k])
        if j + 1 < phases:
            return start_phase(k, j + 1)
        return [
            send(
                totals[phases].at[k, 0, col_at(d)],
                z_in.at[k, d - 1],
                z_s.at[k, d - 1],
                z_r.at[k, d - 1],
                (my_row, col_at(d)),
            )
            for d in range(1, cols)
        ]

    at_quad = quad if split else 0

    def after_cols(k, copies):
        total = totals[phases][k, 0, my_col].astype(jnp.float32)
        for d, copy in enumerate(copies):
            copy.wait_recv()
            total = total + z_in[k, d].astype(jnp.float32)
        gathered[k, core, at_quad] = total.astype(jnp.bfloat16)
        if not split:
            return []
        own = gathered.at[k, core, quad]
        return [
            send(
                own, own, ag_s.at[k, d], ag_r.at[k, d], (((quad + d) % quads) * 2 + core, my_col)
            )
            for d in range(1, quads)
        ]

    def after_quads(k, copies):
        for copy in copies:
            copy.wait_recv()
        own = gathered.at[k, core]
        return send(own, own, ag_s.at[k, 0], ag_r.at[k, 0], sibling)

    scale = 1.0 / math.sqrt(tile_rows * width * rows * cols)

    def finish(k, copy):
        copy.wait_recv()
        for h in range(2):
            first = k * taps + h * half_k
            wg_ref[:, first : first + half_k] = (
                gathered[k, h].astype(jnp.float32).reshape(cs, half_k) * scale
            )

    quarter = tile_rows // 4

    def input_part(b):
        acc = None
        for a in range(3):
            for c in range(3):
                first = b * quarter + 2 - a
                term = jnp.dot(
                    g3[first : first + quarter, :, c * chan : (c + 1) * chan].reshape(
                        quarter * width, out_chan
                    ),
                    wt[:, a * taps + c * chan : a * taps + (c + 1) * chan],
                    preferred_element_type=jnp.float32,
                )
                acc = term if acc is None else acc + term
        igrad_ref[b * quarter : (b + 1) * quarter] = acc.astype(jnp.bfloat16).reshape(
            quarter, width, chan
        )

    flight = [None] * 3
    flight[0] = weight_part(0)
    flight[1] = weight_part(1)
    flight[0] = after_siblings(0, flight[0])
    flight[2] = weight_part(2)
    flight[1] = after_siblings(1, flight[1])
    input_part(1)
    flight[2] = after_siblings(2, flight[2])
    for j in range(phases):
        for k in range(3):
            flight[k] = after_phase(k, j, flight[k])
        if j == 0:
            input_part(2)
    halo_rows(g3, g_halo, g_copies, True)
    input_part(0)
    for k in range(3):
        flight[k] = after_cols(k, flight[k])
    input_part(3)
    for k in range(3):
        flight[k] = after_quads(k, flight[k])
    for k in range(3):
        finish(k, flight[k])

    for copy in started:
        copy.wait_send()
    for up, down in (x_copies, g_copies):

        @pl.when(has_up)
        def _():
            up.wait_send()

        @pl.when(has_down)
        def _():
            down.wait_send()


def on_device(images, weight, norm_gain, cotangent):
    _, tile_rows, width, chan = images.shape
    rows, cols = lax.axis_size("row"), lax.axis_size("col")
    cs = weight.shape[3]
    quads = rows // 2
    split = quads == 4 and cs % 64 == 0
    pieces = quads if split else 1
    rs = cs // pieces
    phases = quads.bit_length() - 1
    out_chan = cs * cols
    taps = 3 * chan
    half = taps // 2
    bf16 = jnp.bfloat16
    vmem = pltpu.VMEM
    dma = pltpu.SemaphoreType.DMA
    counts = [pieces >> j if split else 1 for j in range(phases + 1)]
    scratch = [
        vmem((out_chan, 3 * taps), bf16),
        vmem((tile_rows + 2, width, taps), bf16),
        vmem((tile_rows + 2, width, 3 * out_chan), bf16),
        vmem((out_chan, tile_rows * width), bf16),
        vmem((tile_rows, width, out_chan), jnp.float32),
        vmem((2, width, chan), bf16),
        vmem((2, width, out_chan), bf16),
        vmem((3, 2, pieces, cols, rs, half), bf16),
        vmem((3, pieces, cols, rs, half), bf16),
        vmem((3, 2, pieces, rs, half), bf16),
        vmem((3, cols - 1, rs, half), bf16),
    ]
    scratch += [vmem((3, n, cols, rs, half), bf16) for n in counts]
    scratch += [vmem((3, n, cols, rs, half), bf16) for n in counts[1:]]
    for shape in (
        (4,),
        (cols - 1,),
        (cols - 1, 3),
        (cols - 1,),
        (3, phases + 1),
        (3, cols - 1),
        (3, quads),
    ):
        scratch += [dma(shape), dma(shape)]
    in_vmem = pl.BlockSpec(memory_space=pltpu.VMEM)
    flops = 3 * 2 * tile_rows * width * 3 * taps * out_chan
    features, input_grad, wide_grad = pl.pallas_call(
        functools.partial(kernel, (rows, cols, quads, split, cs, rs)),
        out_shape=(
            jax.ShapeDtypeStruct((tile_rows, width, out_chan), bf16),
            jax.ShapeDtypeStruct((tile_rows, width, chan), bf16),
            jax.ShapeDtypeStruct((cs, 3 * taps), jnp.float32),
        ),
        in_specs=[in_vmem] * 4,
        out_specs=(in_vmem,) * 3,
        scratch_shapes=scratch,
        cost_estimate=pl.CostEstimate(
            flops=flops, bytes_accessed=4 << 20, transcendentals=2 * tile_rows * width * out_chan
        ),
        compiler_params=pltpu.CompilerParams(
            collective_id=0, has_side_effects=True, vmem_limit_bytes=48 << 20
        ),
    )(
        images.reshape(tile_rows, width, chan),
        weight.reshape(3 * taps, cs),
        norm_gain.reshape(1, out_chan),
        cotangent.reshape(tile_rows, width, out_chan),
    )
    weight_grad = wide_grad.T.reshape(3, 3, chan, cs)
    return (features[None], input_grad[None], weight_grad)


def solution(mesh):
    placed = (
        P("row", "col", None, None),
        P(None, None, None, "col"),
        P(),
        P("row", "col", None, None),
    )
    return jax.shard_map(
        on_device,
        mesh=mesh,
        in_specs=placed,
        out_specs=(
            P("row", "col", None, None),
            P("row", "col", None, None),
            P(None, None, None, "col"),
        ),
        check_vma=False,
    )
```

```python
import functools
import math

import jax
import jax.numpy as jnp
from jax import lax
from jax.experimental import pallas as pl
from jax.experimental.pallas import tpu as pltpu
from jax.sharding import PartitionSpec as P

epsilon = 1e-06
root_half = 0.7071067811865476
norm_const = 0.3989422804014327
MESH = pl.DeviceIdType.MESH
NT = (((1,), (1,)), ((), ()))


def norm_act(conv_out, upper, norm_gain):
    mean_val = jnp.mean(conv_out, axis=-1, keepdims=True)
    centred = conv_out - mean_val
    variance = jnp.mean(centred * centred, axis=-1, keepdims=True)
    inv_std = lax.rsqrt(variance + epsilon)
    unit = centred * inv_std
    normed = unit * norm_gain
    cdf_val = 0.5 * (1.0 + lax.erf(normed * root_half))
    density = jnp.exp(-0.5 * normed * normed) * norm_const
    outputs = (normed * cdf_val).astype(jnp.bfloat16)
    upstream = upper.astype(jnp.float32) * (cdf_val + normed * density) * norm_gain
    mean_up = jnp.mean(upstream, axis=-1, keepdims=True)
    mean_cross = jnp.mean(upstream * unit, axis=-1, keepdims=True)
    return (outputs, inv_std * (upstream - mean_up - unit * mean_cross))


def kernel(
    plan,
    x_ref,
    w_ref,
    gain_ref,
    cot_ref,
    feat_ref,
    igrad_ref,
    wg_ref,
    wt,
    x3,
    g3,
    gt,
    conv_even,
    conv_odd,
    g_pad,
    x_own,
    cot_own,
    feat_own,
    igrad_own,
    wg_own,
    x_halo,
    g_halo,
    parts,
    parts_in,
    gathered,
    z_in,
    *rest,
):
    rows, cols, quads, split, cs, rs = plan
    phases = quads.bit_length() - 1
    totals, totals_in = rest[: phases + 1], rest[phases + 1 : 2 * phases + 1]
    (in_sem, out_sem, halo_s, halo_r, wz_s, wz_r, wq_s, wq_r, sib_s, sib_r, ph_s, ph_r, z_s, z_r, ag_s, ag_r) = rest[
        2 * phases + 1 :
    ]
    tile_rows, width, chan = x_ref.shape
    out_chan = cs * cols
    taps = 3 * chan
    half_k = taps // 2
    half_w = 3 * half_k
    my_row, my_col = lax.axis_index("row"), lax.axis_index("col")
    quad, core = my_row // 2, my_row % 2
    sibling = (quad * 2 + 1 - core, my_col)
    bits, partners, partner_quads = [], [], []
    for j in range(phases):
        low, high = 1 << j, 1 << (phases - 1 - j)
        mask = low + core * (high - low)
        bit = (1 - core) * ((quad // low) % 2) + core * ((quad // high) % 2)
        other = quad + mask * (1 - 2 * bit)
        bits.append(bit)
        partner_quads.append(other)
        partners.append((other * 2 + core, my_col))
    started = []

    def send(src, dst, send_sem, recv_sem, device):
        copy = pltpu.make_async_remote_copy(
            src_ref=src,
            dst_ref=dst,
            send_sem=send_sem,
            recv_sem=recv_sem,
            device_id=device,
            device_id_type=MESH,
        )
        copy.start()
        started.append(copy)
        return copy

    def col_at(shift):
        return (my_col + cols + shift) % cols

    barrier = pltpu.get_barrier_semaphore()
    for d in range(1, rows):
        pl.semaphore_signal(
            barrier, inc=1, device_id=((my_row + d) % rows, my_col), device_id_type=MESH
        )
    for d in range(1, cols):
        pl.semaphore_signal(barrier, inc=1, device_id=(my_row, col_at(d)), device_id_type=MESH)

    own_rows = pl.ds(pl.multiple_of(my_col * cs, 16), cs)
    own_copies = []
    for t in range(9):
        own_copies.append(
            pltpu.make_async_copy(
                w_ref.at[t], wt.at[own_rows, t * chan : (t + 1) * chan], in_sem.at[t]
            )
        )
    x_copy = pltpu.make_async_copy(x_ref, x_own, in_sem.at[9])
    cot_copy = pltpu.make_async_copy(cot_ref, cot_own, in_sem.at[10])
    for copy in own_copies + [x_copy, cot_copy]:
        copy.start()
    for copy in own_copies:
        copy.wait()

    pl.semaphore_wait(barrier, rows + cols - 2)

    half_lanes = pl.ds(pl.multiple_of(core * half_w, 128), half_w)

    def piece(col, q):
        start = col * cs + (q * rs if split else 0)
        return wt.at[pl.ds(pl.multiple_of(start, 16), rs), half_lanes]

    wz = [None]
    for d in range(1, cols):
        own = piece(my_col, quad)
        wz.append(send(own, own, wz_s.at[d - 1], wz_r.at[d - 1], (my_row, col_at(d))))

    has_up, has_down = my_col > 0, my_col < cols - 1

    def halo_copies(first, last, into, base):
        up = pltpu.make_async_remote_copy(
            src_ref=first,
            dst_ref=into.at[1],
            send_sem=halo_s.at[base],
            recv_sem=halo_r.at[base],
            device_id=(my_row, col_at(-1)),
            device_id_type=MESH,
        )
        down = pltpu.make_async_remote_copy(
            src_ref=last,
            dst_ref=into.at[0],
            send_sem=halo_s.at[base + 1],
            recv_sem=halo_r.at[base + 1],
            device_id=(my_row, col_at(1)),
            device_id_type=MESH,
        )

        @pl.when(has_up)
        def _():
            up.start()

        @pl.when(has_down)
        def _():
            down.start()

        return up, down

    column = lax.broadcasted_iota(jnp.int32, (width, chan), 0)

    def spread(dst, row, value, flip):
        value = value.astype(jnp.float32)
        left = jnp.where(column == 0, 0.0, pltpu.roll(value, 1, 0))
        right = jnp.where(column == width - 1, 0.0, pltpu.roll(value, width - 1, 0))
        shifted = (right, value, left) if flip else (left, value, right)
        for c in range(3):
            dst[row, :, c * chan : (c + 1) * chan] = shifted[c].astype(jnp.bfloat16)

    def halo_rows(dst, into, copies, flip):
        up, down = copies

        @pl.when(has_up)
        def _():
            down.wait_recv()
            spread(dst, 0, into[0], flip)

        @pl.when(jnp.logical_not(has_up))
        def _():
            dst[0] = jnp.zeros(dst.shape[1:], dst.dtype)

        @pl.when(has_down)
        def _():
            up.wait_recv()
            spread(dst, tile_rows + 1, into[1], flip)

        @pl.when(jnp.logical_not(has_down))
        def _():
            dst[tile_rows + 1] = jnp.zeros(dst.shape[1:], dst.dtype)

    x_copies = halo_copies(x_ref.at[0], x_ref.at[tile_rows - 1], x_halo, 0)

    hops = {}
    if split:
        for d in range(1, cols):
            wz[d].wait_recv()
            got = piece(col_at(-d), quad)
            for j in range(2):
                hops[d, j] = send(got, got, wq_s.at[d - 1, j], wq_r.at[d - 1, j], partners[j])

    x_copy.wait()

    @pl.loop(0, tile_rows)
    def _(i):
        spread(x3, i + 1, x_own[i], False)

    if split:
        for d in range(1, cols):
            hops[d, 0].wait_recv()
            got = piece(col_at(-d), partner_quads[0])
            hops[d, 2] = send(got, got, wq_s.at[d - 1, 2], wq_r.at[d - 1, 2], partners[1])
    halo_rows(x3, x_halo, x_copies, False)
    sib = []
    for d in range(1, cols):
        if split:
            hops[d, 1].wait_recv()
            hops[d, 2].wait_recv()
        else:
            wz[d].wait_recv()
        block = wt.at[pl.ds(pl.multiple_of(col_at(-d) * cs, 16), cs), half_lanes]
        sib.append(send(block, block, sib_s.at[d - 1], sib_r.at[d - 1], sibling))
    for copy in sib:
        copy.wait_recv()

    gain = gain_ref[...]
    quarter = tile_rows // 4
    strip = 32

    def convolve(b, into):
        acc = None
        for a in range(3):
            term = lax.dot_general(
                x3[pl.ds(b * quarter + a, quarter)].reshape(quarter * width, taps),
                wt[:, a * taps : (a + 1) * taps],
                NT,
                preferred_element_type=jnp.float32,
            )
            acc = term if acc is None else acc + term
        into[...] = acc.reshape(quarter, width, out_chan)

    def act(b, source):
        for r in range(quarter):
            i = b * quarter + r
            for first in range(0, width, strip):
                span = slice(first, first + strip)
                outputs, grad_pre = norm_act(source[r, span], cot_own[i, span], gain)
                feat_own[i, span] = outputs
                g_pad[r, 8 + first : 8 + first + strip] = grad_pre
            value = g_pad[r, 8 : 8 + width].astype(jnp.bfloat16)
            g3[i + 1, :, 0:out_chan] = g_pad[r, 9 : 9 + width].astype(jnp.bfloat16)
            g3[i + 1, :, out_chan : 2 * out_chan] = value
            g3[i + 1, :, 2 * out_chan :] = g_pad[r, 7 : 7 + width].astype(jnp.bfloat16)
            gt[:, pl.ds(pl.multiple_of(i * width, 128), width)] = value.T

    g_pad[...] = jnp.zeros(g_pad.shape, g_pad.dtype)
    cot_copy.wait()
    convolve(0, conv_even)

    @pl.loop(0, 2)
    def _(t):
        convolve(2 * t + 1, conv_odd)
        act(2 * t, conv_even)
        convolve(jnp.minimum(2 * t + 2, 3), conv_even)
        act(2 * t + 1, conv_odd)

    feat_copy = pltpu.make_async_copy(feat_own, feat_ref, out_sem.at[0])
    feat_copy.start()

    centre = pl.ds(chan, chan)
    g_copies = halo_copies(g3.at[1, :, centre], g3.at[tile_rows, :, centre], g_halo, 2)

    def weight_part(k):
        acc = jnp.dot(
            gt[...],
            x3[k : k + tile_rows].reshape(tile_rows * width, taps),
            preferred_element_type=jnp.float32,
        ).astype(jnp.bfloat16)
        for h in range(2):
            for s in range(quads if split else 1):
                at = (s % 2) * 2 + s // 2 if split and h == 0 else s
                for c in range(cols):
                    first = c * cs + s * rs
                    parts[k, h, at, c] = acc[first : first + rs, h * half_k : (h + 1) * half_k]
        return send(
            parts.at[k, 1 - core], parts_in.at[k], ph_s.at[k, phases], ph_r.at[k, phases], sibling
        )

    def add(one, two):
        return (one.astype(jnp.float32) + two.astype(jnp.float32)).astype(jnp.bfloat16)

    def start_phase(k, j):
        size = totals_in[j].shape[1]
        source = totals[j].at[k, pl.ds((1 - bits[j]) * size, size)] if split else totals[j].at[k]
        return send(source, totals_in[j].at[k], ph_s.at[k, j], ph_r.at[k, j], partners[j])

    def after_siblings(k, copy):
        copy.wait_recv()
        totals[0][k] = add(parts[k, core], parts_in[k])
        return start_phase(k, 0)

    def after_phase(k, j, copy):
        copy.wait_recv()
        size = totals_in[j].shape[1]
        kept = totals[j][k, pl.ds(bits[j] * size, size)] if split else totals[j][k]
        totals[j + 1][k] = add(kept, totals_in[j][k])
        if j + 1 < phases:
            return start_phase(k, j + 1)
        return [
            send(
                totals[phases].at[k, 0, col_at(d)],
                z_in.at[k, d - 1],
                z_s.at[k, d - 1],
                z_r.at[k, d - 1],
                (my_row, col_at(d)),
            )
            for d in range(1, cols)
        ]

    at_quad = quad if split else 0

    def after_cols(k, copies):
        total = totals[phases][k, 0, my_col].astype(jnp.float32)
        for d, copy in enumerate(copies):
            copy.wait_recv()
            total = total + z_in[k, d].astype(jnp.float32)
        gathered[k, core, at_quad] = total.astype(jnp.bfloat16)
        if not split:
            return []
        own = gathered.at[k, core, quad]
        return [
            send(
                own, own, ag_s.at[k, d], ag_r.at[k, d], (((quad + d) % quads) * 2 + core, my_col)
            )
            for d in range(1, quads)
        ]

    def after_quads(k, copies):
        for copy in copies:
            copy.wait_recv()
        own = gathered.at[k, core]
        return send(own, own, ag_s.at[k, 0], ag_r.at[k, 0], sibling)

    scale = 1.0 / math.sqrt(tile_rows * width * rows * cols)

    def finish(k, copy):
        copy.wait_recv()
        for h in range(2):
            value = gathered[k, h].astype(jnp.float32).reshape(cs, half_k) * scale
            for lane in range(0, half_k, 128):
                tap, at = divmod(h * half_k + lane, chan)
                wg_own[3 * k + tap, :, at : at + 128] = value[:, lane : lane + 128]
        done = pltpu.make_async_copy(
            wg_own.at[3 * k : 3 * k + 3], wg_ref.at[3 * k : 3 * k + 3], out_sem.at[2 + k]
        )
        done.start()
        return done

    def input_part(b):
        acc = None
        for a in range(3):
            for c in range(3):
                first = b * quarter + 2 - a
                term = jnp.dot(
                    g3[first : first + quarter, :, c * chan : (c + 1) * chan].reshape(
                        quarter * width, out_chan
                    ),
                    wt[:, a * taps + c * chan : a * taps + (c + 1) * chan],
                    preferred_element_type=jnp.float32,
                )
                acc = term if acc is None else acc + term
        igrad_own[b * quarter : (b + 1) * quarter] = acc.astype(jnp.bfloat16).reshape(
            quarter, width, chan
        )

    flight = [None] * 3
    flight[0] = weight_part(0)
    flight[1] = weight_part(1)
    flight[0] = after_siblings(0, flight[0])
    flight[2] = weight_part(2)
    flight[1] = after_siblings(1, flight[1])
    input_part(1)
    flight[2] = after_siblings(2, flight[2])
    for j in range(phases):
        for k in range(3):
            flight[k] = after_phase(k, j, flight[k])
        if j == 0:
            input_part(2)
    halo_rows(g3, g_halo, g_copies, True)
    input_part(0)
    for k in range(3):
        flight[k] = after_cols(k, flight[k])
    input_part(3)
    igrad_copy = pltpu.make_async_copy(igrad_own, igrad_ref, out_sem.at[1])
    igrad_copy.start()
    for k in range(3):
        flight[k] = after_quads(k, flight[k])
    for k in range(3):
        flight[k] = finish(k, flight[k])

    for copy in started:
        copy.wait_send()
    for copy in [feat_copy, igrad_copy] + flight:
        copy.wait()
    for up, down in (x_copies, g_copies):

        @pl.when(has_up)
        def _():
            up.wait_send()

        @pl.when(has_down)
        def _():
            down.wait_send()


def move(*refs):
    count = len(refs) // 2
    copies = [
        pltpu.make_async_copy(refs[i], refs[count + i], refs[-1].at[i]) for i in range(count)
    ]
    for copy in copies:
        copy.start()
    for copy in copies:
        copy.wait()


def on_device(images, weight, norm_gain, cotangent):
    _, tile_rows, width, chan = images.shape
    rows, cols = lax.axis_size("row"), lax.axis_size("col")
    cs = weight.shape[3]
    quads = rows // 2
    split = quads == 4 and cs % 64 == 0
    pieces = quads if split else 1
    rs = cs // pieces
    phases = quads.bit_length() - 1
    out_chan = cs * cols
    taps = 3 * chan
    half = taps // 2
    bf16 = jnp.bfloat16
    vmem = pltpu.VMEM
    dma = pltpu.SemaphoreType.DMA
    counts = [pieces >> j if split else 1 for j in range(phases + 1)]
    scratch = [
        vmem((out_chan, 3 * taps), bf16),
        vmem((tile_rows + 2, width, taps), bf16),
        vmem((tile_rows + 2, width, 3 * out_chan), bf16),
        vmem((out_chan, tile_rows * width), bf16),
        vmem((tile_rows // 4, width, out_chan), jnp.float32),
        vmem((tile_rows // 4, width, out_chan), jnp.float32),
        vmem((tile_rows // 4, width + 16, out_chan), jnp.float32),
        vmem((tile_rows, width, chan), bf16),
        vmem((tile_rows, width, out_chan), bf16),
        vmem((tile_rows, width, out_chan), bf16),
        vmem((tile_rows, width, chan), bf16),
        vmem((9, cs, chan), jnp.float32),
        vmem((2, width, chan), bf16),
        vmem((2, width, out_chan), bf16),
        vmem((3, 2, pieces, cols, rs, half), bf16),
        vmem((3, pieces, cols, rs, half), bf16),
        vmem((3, 2, pieces, rs, half), bf16),
        vmem((3, cols - 1, rs, half), bf16),
    ]
    scratch += [vmem((3, n, cols, rs, half), bf16) for n in counts]
    scratch += [vmem((3, n, cols, rs, half), bf16) for n in counts[1:]]
    scratch += [dma((11,)), dma((5,))]
    for shape in (
        (4,),
        (cols - 1,),
        (cols - 1, 3),
        (cols - 1,),
        (3, phases + 1),
        (3, cols - 1),
        (3, quads),
    ):
        scratch += [dma(shape), dma(shape)]
    anywhere = pl.BlockSpec(memory_space=pl.ANY)
    flops = 3 * 2 * tile_rows * width * 3 * taps * out_chan
    shapes = (
        jax.ShapeDtypeStruct((tile_rows, width, out_chan), bf16),
        jax.ShapeDtypeStruct((tile_rows, width, chan), bf16),
        jax.ShapeDtypeStruct((9, cs, chan), jnp.float32),
    )
    results = pl.pallas_call(
        functools.partial(kernel, (rows, cols, quads, split, cs, rs)),
        out_shape=shapes,
        in_specs=[anywhere, anywhere, pl.BlockSpec(memory_space=pltpu.VMEM), anywhere],
        out_specs=(anywhere,) * 3,
        scratch_shapes=scratch,
        cost_estimate=pl.CostEstimate(
            flops=flops, bytes_accessed=4 << 20, transcendentals=2 * tile_rows * width * out_chan
        ),
        compiler_params=pltpu.CompilerParams(
            collective_id=0, has_side_effects=True, vmem_limit_bytes=60 << 20
        ),
    )(
        images.reshape(tile_rows, width, chan),
        jnp.swapaxes(weight, 2, 3).reshape(9, cs, chan),
        norm_gain.reshape(1, out_chan),
        cotangent.reshape(tile_rows, width, out_chan),
    )
    features, input_grad, wide_grad = pl.pallas_call(
        move,
        out_shape=shapes,
        in_specs=[anywhere] * 3,
        out_specs=(anywhere,) * 3,
        scratch_shapes=[dma((3,))],
        compiler_params=pltpu.CompilerParams(vmem_limit_bytes=60 << 20),
    )(*results)
    weight_grad = jnp.swapaxes(wide_grad.reshape(3, 3, cs, chan), 2, 3)
    return (features[None], input_grad[None], weight_grad)


def solution(mesh):
    placed = (
        P("row", "col", None, None),
        P(None, None, None, "col"),
        P(),
        P("row", "col", None, None),
    )
    return jax.shard_map(
        on_device,
        mesh=mesh,
        in_specs=placed,
        out_specs=(
            P("row", "col", None, None),
            P("row", "col", None, None),
            P(None, None, None, "col"),
        ),
        check_vma=False,
    )
```

```python
import functools
import math

import jax
import jax.numpy as jnp
from jax import lax
from jax.experimental import pallas as pl
from jax.experimental.pallas import tpu as pltpu
from jax.sharding import PartitionSpec as P

epsilon = 1e-06
root_half = 0.7071067811865476
norm_const = 0.3989422804014327
MESH = pl.DeviceIdType.MESH
NT = (((1,), (1,)), ((), ()))


def norm_act(conv_out, upper, norm_gain):
    mean_val = jnp.mean(conv_out, axis=-1, keepdims=True)
    centred = conv_out - mean_val
    variance = jnp.mean(centred * centred, axis=-1, keepdims=True)
    inv_std = lax.rsqrt(variance + epsilon)
    unit = centred * inv_std
    normed = unit * norm_gain
    cdf_val = 0.5 * (1.0 + lax.erf(normed * root_half))
    density = jnp.exp(-0.5 * normed * normed) * norm_const
    outputs = (normed * cdf_val).astype(jnp.bfloat16)
    upstream = upper.astype(jnp.float32) * (cdf_val + normed * density) * norm_gain
    mean_up = jnp.mean(upstream, axis=-1, keepdims=True)
    mean_cross = jnp.mean(upstream * unit, axis=-1, keepdims=True)
    return (outputs, inv_std * (upstream - mean_up - unit * mean_cross))


def kernel(
    plan,
    x_ref,
    w_ref,
    gain_ref,
    cot_ref,
    feat_own,
    igrad_own,
    wg_own,
    wt,
    x3,
    g3,
    gt,
    conv_even,
    conv_odd,
    g_pad,
    x_own,
    cot_own,
    x_halo,
    g_halo,
    parts,
    parts_in,
    gathered,
    z_in,
    *rest,
):
    rows, cols, quads, split, cs, rs = plan
    phases = quads.bit_length() - 1
    totals, totals_in = rest[: phases + 1], rest[phases + 1 : 2 * phases + 1]
    (in_sem, halo_s, halo_r, wz_s, wz_r, wq_s, wq_r, sib_s, sib_r, ph_s, ph_r, z_s, z_r, ag_s, ag_r, all_s, all_r) = rest[
        2 * phases + 1 :
    ]
    tile_rows, width, chan = x_ref.shape
    out_chan = cs * cols
    taps = 3 * chan
    half_k = taps // 2
    half_w = 3 * half_k
    my_row, my_col = lax.axis_index("row"), lax.axis_index("col")
    quad, core = my_row // 2, my_row % 2
    sibling = (quad * 2 + 1 - core, my_col)
    bits, partners, partner_quads = [], [], []
    for j in range(phases):
        low, high = 1 << j, 1 << (phases - 1 - j)
        mask = low + core * (high - low)
        bit = (1 - core) * ((quad // low) % 2) + core * ((quad // high) % 2)
        other = quad + mask * (1 - 2 * bit)
        bits.append(bit)
        partner_quads.append(other)
        partners.append((other * 2 + core, my_col))
    started = []

    def send(src, dst, send_sem, recv_sem, device):
        copy = pltpu.make_async_remote_copy(
            src_ref=src,
            dst_ref=dst,
            send_sem=send_sem,
            recv_sem=recv_sem,
            device_id=device,
            device_id_type=MESH,
        )
        copy.start()
        started.append(copy)
        return copy

    def col_at(shift):
        return (my_col + cols + shift) % cols

    barrier = pltpu.get_barrier_semaphore()
    for d in range(1, rows):
        pl.semaphore_signal(
            barrier, inc=1, device_id=((my_row + d) % rows, my_col), device_id_type=MESH
        )
    for d in range(1, cols):
        pl.semaphore_signal(barrier, inc=1, device_id=(my_row, col_at(d)), device_id_type=MESH)

    own_rows = pl.ds(pl.multiple_of(my_col * cs, 16), cs)
    own_copies = []
    for t in range(9):
        own_copies.append(
            pltpu.make_async_copy(
                w_ref.at[t], wt.at[own_rows, t * chan : (t + 1) * chan], in_sem.at[t]
            )
        )
    x_copy = pltpu.make_async_copy(x_ref, x_own, in_sem.at[9])
    cot_copy = pltpu.make_async_copy(cot_ref, cot_own, in_sem.at[10])
    for copy in own_copies + [x_copy, cot_copy]:
        copy.start()
    for copy in own_copies:
        copy.wait()

    pl.semaphore_wait(barrier, rows + cols - 2)

    half_lanes = pl.ds(pl.multiple_of(core * half_w, 128), half_w)

    def piece(col, q):
        start = col * cs + (q * rs if split else 0)
        return wt.at[pl.ds(pl.multiple_of(start, 16), rs), half_lanes]

    def other_col(e):
        first = e + (cols + e - my_col) // cols
        last = cols - 1 - (e + (e + 1 + my_col) // cols)
        far = (2 * my_col) // cols
        return first + far * (last - first)

    own = piece(my_col, quad)
    wz = []
    for e in range(cols - 1):
        to = other_col(e)
        wz.append(
            pltpu.make_async_remote_copy(
                src_ref=own,
                dst_ref=own,
                send_sem=wz_s.at[to],
                recv_sem=wz_r.at[my_col],
                device_id=(my_row, to),
                device_id_type=MESH,
            )
        )
        wz[e].start()

    def arrived(e):
        col = other_col(e)
        got = piece(col, quad)
        pltpu.make_async_copy(got, got, wz_r.at[col]).wait()
        return col, got

    has_up, has_down = my_col > 0, my_col < cols - 1

    def halo_copies(first, last, into, base):
        up = pltpu.make_async_remote_copy(
            src_ref=first,
            dst_ref=into.at[1],
            send_sem=halo_s.at[base],
            recv_sem=halo_r.at[base],
            device_id=(my_row, col_at(-1)),
            device_id_type=MESH,
        )
        down = pltpu.make_async_remote_copy(
            src_ref=last,
            dst_ref=into.at[0],
            send_sem=halo_s.at[base + 1],
            recv_sem=halo_r.at[base + 1],
            device_id=(my_row, col_at(1)),
            device_id_type=MESH,
        )

        @pl.when(has_up)
        def _():
            up.start()

        @pl.when(has_down)
        def _():
            down.start()

        return up, down

    column = lax.broadcasted_iota(jnp.int32, (width, chan), 0)

    def spread(dst, row, value, flip):
        value = value.astype(jnp.float32)
        left = jnp.where(column == 0, 0.0, pltpu.roll(value, 1, 0))
        right = jnp.where(column == width - 1, 0.0, pltpu.roll(value, width - 1, 0))
        shifted = (right, value, left) if flip else (left, value, right)
        for c in range(3):
            dst[row, :, c * chan : (c + 1) * chan] = shifted[c].astype(jnp.bfloat16)

    def halo_rows(dst, into, copies, flip):
        up, down = copies

        @pl.when(has_up)
        def _():
            down.wait_recv()
            spread(dst, 0, into[0], flip)

        @pl.when(jnp.logical_not(has_up))
        def _():
            dst[0] = jnp.zeros(dst.shape[1:], dst.dtype)

        @pl.when(has_down)
        def _():
            up.wait_recv()
            spread(dst, tile_rows + 1, into[1], flip)

        @pl.when(jnp.logical_not(has_down))
        def _():
            dst[tile_rows + 1] = jnp.zeros(dst.shape[1:], dst.dtype)

    x_copies = halo_copies(x_ref.at[0], x_ref.at[tile_rows - 1], x_halo, 0)

    hops = {}

    def pass_on(e):
        col, got = arrived(e)
        for j in range(2):
            hops[e, j] = send(got, got, wq_s.at[e, j], wq_r.at[e, j], partners[j])

    def pass_again(e):
        hops[e, 0].wait_recv()
        got = piece(other_col(e), partner_quads[0])
        hops[e, 2] = send(got, got, wq_s.at[e, 2], wq_r.at[e, 2], partners[1])

    sib = []

    def to_sibling(e):
        if split:
            hops[e, 1].wait_recv()
            hops[e, 2].wait_recv()
            col = other_col(e)
        else:
            col, _ = arrived(e)
        block = wt.at[pl.ds(pl.multiple_of(col * cs, 16), cs), half_lanes]
        sib.append(send(block, block, sib_s.at[e], sib_r.at[e], sibling))

    def spread_rows(first, last):
        @pl.loop(first, last)
        def _(i):
            spread(x3, i + 1, x_own[i], False)

    x_copy.wait()
    steps = cols - 1
    cut = tile_rows // 4
    spread_rows(0, cut)
    if split:
        pass_on(0)
        spread_rows(cut, 2 * cut)
        for e in range(1, steps):
            pass_on(e)
            pass_again(e - 1)
            if e > 1:
                to_sibling(e - 2)
        pass_again(steps - 1)
        for e in range(max(steps - 2, 0), steps - 1):
            to_sibling(e)
        spread_rows(2 * cut, tile_rows)
        halo_rows(x3, x_halo, x_copies, False)
        to_sibling(steps - 1)
    else:
        spread_rows(cut, tile_rows)
        for e in range(steps):
            to_sibling(e)
        halo_rows(x3, x_halo, x_copies, False)
    for copy in sib:
        copy.wait_recv()

    gain = gain_ref[...]
    quarter = tile_rows // 4
    strip = 32

    def convolve(b, into):
        acc = None
        for a in range(3):
            term = lax.dot_general(
                x3[pl.ds(b * quarter + a, quarter)].reshape(quarter * width, taps),
                wt[:, a * taps : (a + 1) * taps],
                NT,
                preferred_element_type=jnp.float32,
            )
            acc = term if acc is None else acc + term
        into[...] = acc.reshape(quarter, width, out_chan)

    def act(b, source):
        for r in range(quarter):
            i = b * quarter + r
            for first in range(0, width, strip):
                span = slice(first, first + strip)
                outputs, grad_pre = norm_act(source[r, span], cot_own[i, span], gain)
                feat_own[i, span] = outputs
                g_pad[r, 8 + first : 8 + first + strip] = grad_pre
            value = g_pad[r, 8 : 8 + width].astype(jnp.bfloat16)
            g3[i + 1, :, 0:out_chan] = g_pad[r, 9 : 9 + width].astype(jnp.bfloat16)
            g3[i + 1, :, out_chan : 2 * out_chan] = value
            g3[i + 1, :, 2 * out_chan :] = g_pad[r, 7 : 7 + width].astype(jnp.bfloat16)
            gt[:, pl.ds(pl.multiple_of(i * width, 128), width)] = value.T

    g_pad[...] = jnp.zeros(g_pad.shape, g_pad.dtype)
    cot_copy.wait()
    convolve(0, conv_even)

    @pl.loop(0, 2)
    def _(t):
        convolve(2 * t + 1, conv_odd)
        act(2 * t, conv_even)
        convolve(jnp.minimum(2 * t + 2, 3), conv_even)
        act(2 * t + 1, conv_odd)

    centre = pl.ds(chan, chan)
    g_copies = halo_copies(g3.at[1, :, centre], g3.at[tile_rows, :, centre], g_halo, 2)

    def weight_part(k):
        acc = jnp.dot(
            gt[...],
            x3[k : k + tile_rows].reshape(tile_rows * width, taps),
            preferred_element_type=jnp.float32,
        ).astype(jnp.bfloat16)
        for h in range(2):
            for s in range(quads if split else 1):
                at = (s % 2) * 2 + s // 2 if split and h == 0 else s
                for c in range(cols):
                    first = c * cs + s * rs
                    parts[k, h, at, c] = acc[first : first + rs, h * half_k : (h + 1) * half_k]
        return send(
            parts.at[k, 1 - core], parts_in.at[k], ph_s.at[k, phases], ph_r.at[k, phases], sibling
        )

    def add(one, two):
        return (one.astype(jnp.float32) + two.astype(jnp.float32)).astype(jnp.bfloat16)

    def start_phase(k, j):
        size = totals_in[j].shape[1]
        source = totals[j].at[k, pl.ds((1 - bits[j]) * size, size)] if split else totals[j].at[k]
        return send(source, totals_in[j].at[k], ph_s.at[k, j], ph_r.at[k, j], partners[j])

    def after_siblings(k, copy):
        copy.wait_recv()
        totals[0][k] = add(parts[k, core], parts_in[k])
        return start_phase(k, 0)

    def after_phase(k, j, copy):
        copy.wait_recv()
        size = totals_in[j].shape[1]
        kept = totals[j][k, pl.ds(bits[j] * size, size)] if split else totals[j][k]
        totals[j + 1][k] = add(kept, totals_in[j][k])
        if j + 1 < phases:
            return start_phase(k, j + 1)
        return [
            send(
                totals[phases].at[k, 0, col_at(d)],
                z_in.at[k, d - 1],
                z_s.at[k, d - 1],
                z_r.at[k, d - 1],
                (my_row, col_at(d)),
            )
            for d in range(1, cols)
        ]

    at_quad = quad if split else 0

    def after_cols(k, copies):
        total = totals[phases][k, 0, my_col].astype(jnp.float32)
        for d, copy in enumerate(copies):
            copy.wait_recv()
            total = total + z_in[k, d].astype(jnp.float32)
        gathered[k, core, at_quad] = total.astype(jnp.bfloat16)
        if not split:
            return []
        own = gathered.at[k, core, quad]
        if k == 2:
            return [
                send(
                    own,
                    own,
                    all_s.at[d - 1],
                    all_r.at[my_row],
                    ((my_row + d) % rows, my_col),
                )
                for d in range(1, rows)
            ]
        return [
            send(
                own, own, ag_s.at[k, d], ag_r.at[k, d], (((quad + d) % quads) * 2 + core, my_col)
            )
            for d in range(1, quads)
        ]

    def after_quads(k, copies):
        if split and k == 2:
            for d in range(1, rows):
                row = (my_row + d) % rows
                got = gathered.at[k, row % 2, row // 2]
                pltpu.make_async_copy(got, got, all_r.at[row]).wait()
            return None
        for copy in copies:
            copy.wait_recv()
        own = gathered.at[k, core]
        return send(own, own, ag_s.at[k, 0], ag_r.at[k, 0], sibling)

    scale = 1.0 / math.sqrt(tile_rows * width * rows * cols)

    def finish(k, copy):
        if copy is not None:
            copy.wait_recv()
        for h in range(2):
            value = gathered[k, h].astype(jnp.float32).reshape(cs, half_k) * scale
            for lane in range(0, half_k, 128):
                tap, at = divmod(h * half_k + lane, chan)
                wg_own[3 * k + tap, :, at : at + 128] = value[:, lane : lane + 128]

    def input_part(b):
        acc = None
        for a in range(3):
            for c in range(3):
                first = b * quarter + 2 - a
                term = jnp.dot(
                    g3[first : first + quarter, :, c * chan : (c + 1) * chan].reshape(
                        quarter * width, out_chan
                    ),
                    wt[:, a * taps + c * chan : a * taps + (c + 1) * chan],
                    preferred_element_type=jnp.float32,
                )
                acc = term if acc is None else acc + term
        igrad_own[b * quarter : (b + 1) * quarter] = acc.astype(jnp.bfloat16).reshape(
            quarter, width, chan
        )

    flight = [None] * 3
    flight[0] = weight_part(0)
    flight[1] = weight_part(1)
    flight[0] = after_siblings(0, flight[0])
    flight[2] = weight_part(2)
    flight[1] = after_siblings(1, flight[1])
    flight[0] = after_phase(0, 0, flight[0])
    flight[2] = after_siblings(2, flight[2])
    input_part(1)
    flight[1] = after_phase(1, 0, flight[1])
    for j in range(1, phases):
        flight[0] = after_phase(0, j, flight[0])
    flight[2] = after_phase(2, 0, flight[2])
    input_part(2)
    for j in range(1, phases):
        flight[1] = after_phase(1, j, flight[1])
    flight[0] = after_cols(0, flight[0])
    for j in range(1, phases):
        flight[2] = after_phase(2, j, flight[2])
    halo_rows(g3, g_halo, g_copies, True)
    input_part(0)
    flight[1] = after_cols(1, flight[1])
    flight[0] = after_quads(0, flight[0])
    flight[2] = after_cols(2, flight[2])
    input_part(3)
    flight[1] = after_quads(1, flight[1])
    finish(0, flight[0])
    finish(1, flight[1])
    flight[2] = after_quads(2, flight[2])
    finish(2, flight[2])

    for copy in started + wz:
        copy.wait_send()
    for up, down in (x_copies, g_copies):

        @pl.when(has_up)
        def _():
            up.wait_send()

        @pl.when(has_down)
        def _():
            down.wait_send()


def move(*refs):
    count = len(refs) // 2
    copies = [
        pltpu.make_async_copy(refs[i], refs[count + i], refs[-1].at[i]) for i in range(count)
    ]
    for copy in copies:
        copy.start()
    for copy in copies:
        copy.wait()


def on_device(images, weight, norm_gain, cotangent):
    _, tile_rows, width, chan = images.shape
    rows, cols = lax.axis_size("row"), lax.axis_size("col")
    cs = weight.shape[3]
    quads = rows // 2
    split = quads == 4 and cs % 64 == 0
    pieces = quads if split else 1
    rs = cs // pieces
    phases = quads.bit_length() - 1
    out_chan = cs * cols
    taps = 3 * chan
    half = taps // 2
    bf16 = jnp.bfloat16
    vmem = pltpu.VMEM
    dma = pltpu.SemaphoreType.DMA
    counts = [pieces >> j if split else 1 for j in range(phases + 1)]
    scratch = [
        vmem((out_chan, 3 * taps), bf16),
        vmem((tile_rows + 2, width, taps), bf16),
        vmem((tile_rows + 2, width, 3 * out_chan), bf16),
        vmem((out_chan, tile_rows * width), bf16),
        vmem((tile_rows // 4, width, out_chan), jnp.float32),
        vmem((tile_rows // 4, width, out_chan), jnp.float32),
        vmem((tile_rows // 4, width + 16, out_chan), jnp.float32),
        vmem((tile_rows, width, chan), bf16),
        vmem((tile_rows, width, out_chan), bf16),
        vmem((2, width, chan), bf16),
        vmem((2, width, out_chan), bf16),
        vmem((3, 2, pieces, cols, rs, half), bf16),
        vmem((3, pieces, cols, rs, half), bf16),
        vmem((3, 2, pieces, rs, half), bf16),
        vmem((3, cols - 1, rs, half), bf16),
    ]
    scratch += [vmem((3, n, cols, rs, half), bf16) for n in counts]
    scratch += [vmem((3, n, cols, rs, half), bf16) for n in counts[1:]]
    scratch += [dma((11,))]
    for shape in (
        (4,),
        (cols,),
        (cols - 1, 3),
        (cols - 1,),
        (3, phases + 1),
        (3, cols - 1),
        (3, quads),
        (rows,),
    ):
        scratch += [dma(shape), dma(shape)]
    in_hbm = pl.BlockSpec(memory_space=pltpu.HBM)
    in_vmem = pl.BlockSpec(memory_space=pltpu.VMEM)
    flops = 3 * 2 * tile_rows * width * 3 * taps * out_chan
    shapes = (
        jax.ShapeDtypeStruct((tile_rows, width, out_chan), bf16),
        jax.ShapeDtypeStruct((tile_rows, width, chan), bf16),
        jax.ShapeDtypeStruct((9, cs, chan), jnp.float32),
    )
    results = pl.pallas_call(
        functools.partial(kernel, (rows, cols, quads, split, cs, rs)),
        out_shape=shapes,
        in_specs=[in_hbm, in_hbm, in_vmem, in_hbm],
        out_specs=(in_vmem,) * 3,
        scratch_shapes=scratch,
        cost_estimate=pl.CostEstimate(
            flops=flops, bytes_accessed=4 << 20, transcendentals=2 * tile_rows * width * out_chan
        ),
        compiler_params=pltpu.CompilerParams(
            collective_id=0, has_side_effects=True, vmem_limit_bytes=48 << 20
        ),
    )(
        images.reshape(tile_rows, width, chan),
        jnp.swapaxes(weight, 2, 3).reshape(9, cs, chan),
        norm_gain.reshape(1, out_chan),
        cotangent.reshape(tile_rows, width, out_chan),
    )
    features, input_grad, wide_grad = pl.pallas_call(
        move,
        out_shape=shapes,
        in_specs=[in_vmem] * 3,
        out_specs=(in_hbm,) * 3,
        scratch_shapes=[dma((3,))],
    )(*results)
    weight_grad = jnp.swapaxes(wide_grad.reshape(3, 3, cs, chan), 2, 3)
    return (features[None], input_grad[None], weight_grad)


def solution(mesh):
    placed = (
        P("row", "col", None, None),
        P(None, None, None, "col"),
        P(),
        P("row", "col", None, None),
    )
    return jax.shard_map(
        on_device,
        mesh=mesh,
        in_specs=placed,
        out_specs=(
            P("row", "col", None, None),
            P("row", "col", None, None),
            P(None, None, None, "col"),
        ),
        check_vma=False,
    )
```

```python
import functools
import math

import jax
import jax.numpy as jnp
from jax import lax
from jax.experimental import pallas as pl
from jax.experimental.pallas import tpu as pltpu
from jax.sharding import PartitionSpec as P

epsilon = 1e-06
root_half = 0.7071067811865476
norm_const = 0.3989422804014327
MESH = pl.DeviceIdType.MESH
NT = (((1,), (1,)), ((), ()))


def norm_act(conv_out, upper, norm_gain):
    mean_val = jnp.mean(conv_out, axis=-1, keepdims=True)
    centred = conv_out - mean_val
    variance = jnp.mean(centred * centred, axis=-1, keepdims=True)
    inv_std = lax.rsqrt(variance + epsilon)
    unit = centred * inv_std
    normed = unit * norm_gain
    cdf_val = 0.5 * (1.0 + lax.erf(normed * root_half))
    density = jnp.exp(-0.5 * normed * normed) * norm_const
    outputs = (normed * cdf_val).astype(jnp.bfloat16)
    upstream = upper.astype(jnp.float32) * (cdf_val + normed * density) * norm_gain
    mean_up = jnp.mean(upstream, axis=-1, keepdims=True)
    mean_cross = jnp.mean(upstream * unit, axis=-1, keepdims=True)
    return (outputs, inv_std * (upstream - mean_up - unit * mean_cross))


def kernel(
    plan,
    x_ref,
    w_ref,
    gain_ref,
    cot_ref,
    feat_ref,
    igrad_ref,
    wg_ref,
    wt,
    x3,
    g3,
    gt,
    conv,
    g_pad,
    x_own,
    cot_own,
    feat_own,
    igrad_own,
    wg_own,
    x_halo,
    g_halo,
    parts,
    parts_in,
    gathered,
    z_in,
    *rest,
):
    rows, cols, quads, split, cs, rs = plan
    phases = quads.bit_length() - 1
    totals, totals_in = rest[: phases + 1], rest[phases + 1 : 2 * phases + 1]
    (in_sem, out_sem, halo_s, halo_r, wz_s, wz_r, wq_s, wq_r, sib_s, sib_r, ph_s, ph_r, z_s, z_r, ag_s, ag_r, all_s, all_r) = rest[
        2 * phases + 1 :
    ]
    tile_rows, width, chan = x_ref.shape
    out_chan = cs * cols
    taps = 3 * chan
    half_k = taps // 2
    half_w = 3 * half_k
    my_row, my_col = lax.axis_index("row"), lax.axis_index("col")
    quad, core = my_row // 2, my_row % 2
    sibling = (quad * 2 + 1 - core, my_col)
    bits, partners, partner_quads = [], [], []
    for j in range(phases):
        low, high = 1 << j, 1 << (phases - 1 - j)
        mask = low + core * (high - low)
        bit = (1 - core) * ((quad // low) % 2) + core * ((quad // high) % 2)
        other = quad + mask * (1 - 2 * bit)
        bits.append(bit)
        partner_quads.append(other)
        partners.append((other * 2 + core, my_col))
    started = []

    def send(src, dst, send_sem, recv_sem, device):
        copy = pltpu.make_async_remote_copy(
            src_ref=src,
            dst_ref=dst,
            send_sem=send_sem,
            recv_sem=recv_sem,
            device_id=device,
            device_id_type=MESH,
        )
        copy.start()
        started.append(copy)
        return copy

    def col_at(shift):
        return (my_col + cols + shift) % cols

    barrier = pltpu.get_barrier_semaphore()
    for d in range(1, rows):
        pl.semaphore_signal(
            barrier, inc=1, device_id=((my_row + d) % rows, my_col), device_id_type=MESH
        )
    for d in range(1, cols):
        pl.semaphore_signal(barrier, inc=1, device_id=(my_row, col_at(d)), device_id_type=MESH)

    own_rows = pl.ds(pl.multiple_of(my_col * cs, 16), cs)
    own_copies = []
    for t in range(9):
        own_copies.append(
            pltpu.make_async_copy(
                w_ref.at[t], wt.at[own_rows, t * chan : (t + 1) * chan], in_sem.at[t]
            )
        )
    x_copy = pltpu.make_async_copy(x_ref, x_own, in_sem.at[9])
    cot_copy = pltpu.make_async_copy(cot_ref, cot_own, in_sem.at[10])
    for copy in own_copies + [x_copy, cot_copy]:
        copy.start()
    for copy in own_copies:
        copy.wait()

    pl.semaphore_wait(barrier, rows + cols - 2)

    half_lanes = pl.ds(pl.multiple_of(core * half_w, 128), half_w)

    def piece(col, q):
        start = col * cs + (q * rs if split else 0)
        return wt.at[pl.ds(pl.multiple_of(start, 16), rs), half_lanes]

    def other_col(e):
        first = e + (cols + e - my_col) // cols
        last = cols - 1 - (e + (e + 1 + my_col) // cols)
        far = (2 * my_col) // cols
        return first + far * (last - first)

    own = piece(my_col, quad)
    wz = []
    for e in range(cols - 1):
        to = other_col(e)
        wz.append(
            pltpu.make_async_remote_copy(
                src_ref=own,
                dst_ref=own,
                send_sem=wz_s.at[to],
                recv_sem=wz_r.at[my_col],
                device_id=(my_row, to),
                device_id_type=MESH,
            )
        )
        wz[e].start()

    def arrived(e):
        col = other_col(e)
        got = piece(col, quad)
        pltpu.make_async_copy(got, got, wz_r.at[col]).wait()
        return col, got

    has_up, has_down = my_col > 0, my_col < cols - 1

    def halo_copies(first, last, into, base):
        up = pltpu.make_async_remote_copy(
            src_ref=first,
            dst_ref=into.at[1],
            send_sem=halo_s.at[base],
            recv_sem=halo_r.at[base],
            device_id=(my_row, col_at(-1)),
            device_id_type=MESH,
        )
        down = pltpu.make_async_remote_copy(
            src_ref=last,
            dst_ref=into.at[0],
            send_sem=halo_s.at[base + 1],
            recv_sem=halo_r.at[base + 1],
            device_id=(my_row, col_at(1)),
            device_id_type=MESH,
        )

        @pl.when(has_up)
        def _():
            up.start()

        @pl.when(has_down)
        def _():
            down.start()

        return up, down

    column = lax.broadcasted_iota(jnp.int32, (width, chan), 0)

    def spread(dst, row, value, flip):
        value = value.astype(jnp.float32)
        left = jnp.where(column == 0, 0.0, pltpu.roll(value, 1, 0))
        right = jnp.where(column == width - 1, 0.0, pltpu.roll(value, width - 1, 0))
        shifted = (right, value, left) if flip else (left, value, right)
        for c in range(3):
            dst[row, :, c * chan : (c + 1) * chan] = shifted[c].astype(jnp.bfloat16)

    def halo_rows(dst, into, copies, flip):
        up, down = copies

        @pl.when(has_up)
        def _():
            down.wait_recv()
            spread(dst, 0, into[0], flip)

        @pl.when(jnp.logical_not(has_up))
        def _():
            dst[0] = jnp.zeros(dst.shape[1:], dst.dtype)

        @pl.when(has_down)
        def _():
            up.wait_recv()
            spread(dst, tile_rows + 1, into[1], flip)

        @pl.when(jnp.logical_not(has_down))
        def _():
            dst[tile_rows + 1] = jnp.zeros(dst.shape[1:], dst.dtype)

    x_copies = halo_copies(x_ref.at[0], x_ref.at[tile_rows - 1], x_halo, 0)

    hops = {}

    def pass_on(e):
        col, got = arrived(e)
        for j in range(2):
            hops[e, j] = send(got, got, wq_s.at[e, j], wq_r.at[e, j], partners[j])

    def pass_again(e):
        hops[e, 0].wait_recv()
        got = piece(other_col(e), partner_quads[0])
        hops[e, 2] = send(got, got, wq_s.at[e, 2], wq_r.at[e, 2], partners[1])

    sib = []

    def to_sibling(e):
        if split:
            hops[e, 1].wait_recv()
            hops[e, 2].wait_recv()
            col = other_col(e)
        else:
            col, _ = arrived(e)
        block = wt.at[pl.ds(pl.multiple_of(col * cs, 16), cs), half_lanes]
        sib.append(send(block, block, sib_s.at[e], sib_r.at[e], sibling))

    def spread_rows(first, last):
        @pl.loop(first, last)
        def _(i):
            spread(x3, i + 1, x_own[i], False)

    x_copy.wait()
    steps = cols - 1
    cut = tile_rows // 4
    spread_rows(0, cut)
    if split:
        pass_on(0)
        spread_rows(cut, 2 * cut)
        for e in range(1, steps):
            pass_on(e)
            pass_again(e - 1)
            if e > 1:
                to_sibling(e - 2)
        pass_again(steps - 1)
        for e in range(max(steps - 2, 0), steps - 1):
            to_sibling(e)
        spread_rows(2 * cut, tile_rows)
        halo_rows(x3, x_halo, x_copies, False)
        to_sibling(steps - 1)
    else:
        spread_rows(cut, tile_rows)
        for e in range(steps):
            to_sibling(e)
        halo_rows(x3, x_halo, x_copies, False)
    for copy in sib:
        copy.wait_recv()

    gain = gain_ref[...]
    part_rows = tile_rows // 2
    strip = 32

    @pl.loop(0, 2)
    def _(b):
        acc = None
        for a in range(3):
            term = lax.dot_general(
                x3[pl.ds(b * part_rows + a, part_rows)].reshape(part_rows * width, taps),
                wt[:, a * taps : (a + 1) * taps],
                NT,
                preferred_element_type=jnp.float32,
            )
            acc = term if acc is None else acc + term
        conv[pl.ds(b * part_rows, part_rows)] = acc.reshape(part_rows, width, out_chan)

    g_pad[...] = jnp.zeros(g_pad.shape, g_pad.dtype)
    cot_copy.wait()

    @pl.loop(0, tile_rows)
    def _(i):
        for first in range(0, width, strip):
            span = slice(first, first + strip)
            outputs, grad_pre = norm_act(conv[i, span], cot_own[i, span], gain)
            feat_own[i, span] = outputs
            g_pad[8 + first : 8 + first + strip] = grad_pre
        value = g_pad[8 : 8 + width].astype(jnp.bfloat16)
        g3[i + 1, :, 0:out_chan] = g_pad[9 : 9 + width].astype(jnp.bfloat16)
        g3[i + 1, :, out_chan : 2 * out_chan] = value
        g3[i + 1, :, 2 * out_chan :] = g_pad[7 : 7 + width].astype(jnp.bfloat16)
        gt[:, pl.ds(pl.multiple_of(i * width, 128), width)] = value.T

    feat_copy = pltpu.make_async_copy(feat_own, feat_ref, out_sem.at[0])
    feat_copy.start()

    centre = pl.ds(chan, chan)
    g_copies = halo_copies(g3.at[1, :, centre], g3.at[tile_rows, :, centre], g_halo, 2)

    def to_pair(k):
        return pltpu.make_async_remote_copy(
            src_ref=parts.at[k, 1 - core],
            dst_ref=parts_in.at[k],
            send_sem=ph_s.at[k, phases],
            recv_sem=ph_r.at[k, phases],
            device_id=sibling,
            device_id_type=MESH,
        )

    @pl.loop(0, 3)
    def _(k):
        acc = jnp.dot(
            gt[...],
            x3[pl.ds(k, tile_rows)].reshape(tile_rows * width, taps),
            preferred_element_type=jnp.float32,
        ).astype(jnp.bfloat16)
        for h in range(2):
            for s in range(quads if split else 1):
                at = (s % 2) * 2 + s // 2 if split and h == 0 else s
                for c in range(cols):
                    first = c * cs + s * rs
                    parts[k, h, at, c] = acc[first : first + rs, h * half_k : (h + 1) * half_k]
        to_pair(k).start()

    def add(one, two):
        return (one.astype(jnp.float32) + two.astype(jnp.float32)).astype(jnp.bfloat16)

    def start_phase(k, j):
        size = totals_in[j].shape[1]
        source = totals[j].at[k, pl.ds((1 - bits[j]) * size, size)] if split else totals[j].at[k]
        return send(source, totals_in[j].at[k], ph_s.at[k, j], ph_r.at[k, j], partners[j])

    def after_siblings(k, copy):
        copy.wait_recv()
        totals[0][k] = add(parts[k, core], parts_in[k])
        return start_phase(k, 0)

    def after_phase(k, j, copy):
        copy.wait_recv()
        size = totals_in[j].shape[1]
        kept = totals[j][k, pl.ds(bits[j] * size, size)] if split else totals[j][k]
        totals[j + 1][k] = add(kept, totals_in[j][k])
        if j + 1 < phases:
            return start_phase(k, j + 1)
        return [
            send(
                totals[phases].at[k, 0, col_at(d)],
                z_in.at[k, d - 1],
                z_s.at[k, d - 1],
                z_r.at[k, d - 1],
                (my_row, col_at(d)),
            )
            for d in range(1, cols)
        ]

    at_quad = quad if split else 0

    def after_cols(k, copies):
        total = totals[phases][k, 0, my_col].astype(jnp.float32)
        for d, copy in enumerate(copies):
            copy.wait_recv()
            total = total + z_in[k, d].astype(jnp.float32)
        gathered[k, core, at_quad] = total.astype(jnp.bfloat16)
        if not split:
            return []
        own = gathered.at[k, core, quad]
        if k == 2:
            return [
                send(
                    own,
                    own,
                    all_s.at[d - 1],
                    all_r.at[my_row],
                    ((my_row + d) % rows, my_col),
                )
                for d in range(1, rows)
            ]
        return [
            send(
                own, own, ag_s.at[k, d], ag_r.at[k, d], (((quad + d) % quads) * 2 + core, my_col)
            )
            for d in range(1, quads)
        ]

    def after_quads(k, copies):
        if split and k == 2:
            for d in range(1, rows):
                row = (my_row + d) % rows
                got = gathered.at[k, row % 2, row // 2]
                pltpu.make_async_copy(got, got, all_r.at[row]).wait()
            return None
        for copy in copies:
            copy.wait_recv()
        own = gathered.at[k, core]
        return send(own, own, ag_s.at[k, 0], ag_r.at[k, 0], sibling)

    scale = 1.0 / math.sqrt(tile_rows * width * rows * cols)

    def finish(k, copy):
        if copy is not None:
            copy.wait_recv()
        for h in range(2):
            value = gathered[k, h].astype(jnp.float32).reshape(cs, half_k) * scale
            for lane in range(0, half_k, 128):
                tap, at = divmod(h * half_k + lane, chan)
                wg_own[3 * k + tap, :, at : at + 128] = value[:, lane : lane + 128]
        done = pltpu.make_async_copy(
            wg_own.at[3 * k : 3 * k + 3], wg_ref.at[3 * k : 3 * k + 3], out_sem.at[2 + k]
        )
        done.start()
        return done

    def input_part(b):
        acc = None
        for a in range(3):
            for c in range(3):
                first = b * part_rows + 2 - a
                term = jnp.dot(
                    g3[first : first + part_rows, :, c * chan : (c + 1) * chan].reshape(
                        part_rows * width, out_chan
                    ),
                    wt[:, a * taps + c * chan : a * taps + (c + 1) * chan],
                    preferred_element_type=jnp.float32,
                )
                acc = term if acc is None else acc + term
        igrad_own[b * part_rows : (b + 1) * part_rows] = acc.astype(jnp.bfloat16).reshape(
            part_rows, width, chan
        )

    flight = [to_pair(k) for k in range(3)]
    started.extend(flight)
    for k in range(3):
        flight[k] = after_siblings(k, flight[k])
    halo_rows(g3, g_halo, g_copies, True)
    flight[0] = after_phase(0, 0, flight[0])
    flight[1] = after_phase(1, 0, flight[1])
    input_part(0)
    for j in range(1, phases):
        flight[0] = after_phase(0, j, flight[0])
    flight[2] = after_phase(2, 0, flight[2])
    for j in range(1, phases):
        flight[1] = after_phase(1, j, flight[1])
    flight[0] = after_cols(0, flight[0])
    for j in range(1, phases):
        flight[2] = after_phase(2, j, flight[2])
    flight[1] = after_cols(1, flight[1])
    input_part(1)
    igrad_copy = pltpu.make_async_copy(igrad_own, igrad_ref, out_sem.at[1])
    igrad_copy.start()
    flight[0] = after_quads(0, flight[0])
    flight[2] = after_cols(2, flight[2])
    flight[1] = after_quads(1, flight[1])
    flight[0] = finish(0, flight[0])
    flight[1] = finish(1, flight[1])
    flight[2] = after_quads(2, flight[2])
    flight[2] = finish(2, flight[2])

    for copy in started + wz:
        copy.wait_send()
    for copy in [feat_copy, igrad_copy] + flight:
        copy.wait()
    for up, down in (x_copies, g_copies):

        @pl.when(has_up)
        def _():
            up.wait_send()

        @pl.when(has_down)
        def _():
            down.wait_send()


def on_device(images, weight, norm_gain, cotangent):
    _, tile_rows, width, chan = images.shape
    rows, cols = lax.axis_size("row"), lax.axis_size("col")
    cs = weight.shape[3]
    quads = rows // 2
    split = quads == 4 and cs % 64 == 0
    pieces = quads if split else 1
    rs = cs // pieces
    phases = quads.bit_length() - 1
    out_chan = cs * cols
    taps = 3 * chan
    half = taps // 2
    bf16 = jnp.bfloat16
    vmem = pltpu.VMEM
    dma = pltpu.SemaphoreType.DMA
    counts = [pieces >> j if split else 1 for j in range(phases + 1)]
    scratch = [
        vmem((out_chan, 3 * taps), bf16),
        vmem((tile_rows + 2, width, taps), bf16),
        vmem((tile_rows + 2, width, 3 * out_chan), bf16),
        vmem((out_chan, tile_rows * width), bf16),
        vmem((tile_rows, width, out_chan), jnp.float32),
        vmem((width + 16, out_chan), jnp.float32),
        vmem((tile_rows, width, chan), bf16),
        vmem((tile_rows, width, out_chan), bf16),
        vmem((tile_rows, width, out_chan), bf16),
        vmem((tile_rows, width, chan), bf16),
        vmem((9, cs, chan), jnp.float32),
        vmem((2, width, chan), bf16),
        vmem((2, width, out_chan), bf16),
        vmem((3, 2, pieces, cols, rs, half), bf16),
        vmem((3, pieces, cols, rs, half), bf16),
        vmem((3, 2, pieces, rs, half), bf16),
        vmem((3, cols - 1, rs, half), bf16),
    ]
    scratch += [vmem((3, n, cols, rs, half), bf16) for n in counts]
    scratch += [vmem((3, n, cols, rs, half), bf16) for n in counts[1:]]
    scratch += [dma((11,)), dma((5,))]
    for shape in (
        (4,),
        (cols,),
        (cols - 1, 3),
        (cols - 1,),
        (3, phases + 1),
        (3, cols - 1),
        (3, quads),
        (rows,),
    ):
        scratch += [dma(shape), dma(shape)]
    in_hbm = pl.BlockSpec(memory_space=pltpu.HBM)
    in_vmem = pl.BlockSpec(memory_space=pltpu.VMEM)
    flops = 3 * 2 * tile_rows * width * 3 * taps * out_chan
    shapes = (
        jax.ShapeDtypeStruct((tile_rows, width, out_chan), bf16),
        jax.ShapeDtypeStruct((tile_rows, width, chan), bf16),
        jax.ShapeDtypeStruct((9, cs, chan), jnp.float32),
    )
    features, input_grad, wide_grad = pl.pallas_call(
        functools.partial(kernel, (rows, cols, quads, split, cs, rs)),
        out_shape=shapes,
        in_specs=[in_hbm, in_hbm, in_vmem, in_hbm],
        out_specs=(in_hbm,) * 3,
        scratch_shapes=scratch,
        cost_estimate=pl.CostEstimate(
            flops=flops, bytes_accessed=4 << 20, transcendentals=2 * tile_rows * width * out_chan
        ),
        compiler_params=pltpu.CompilerParams(
            collective_id=0, has_side_effects=True, vmem_limit_bytes=60 << 20
        ),
    )(
        images.reshape(tile_rows, width, chan),
        jnp.swapaxes(weight, 2, 3).reshape(9, cs, chan),
        norm_gain.reshape(1, out_chan),
        cotangent.reshape(tile_rows, width, out_chan),
    )
    weight_grad = jnp.swapaxes(wide_grad.reshape(3, 3, cs, chan), 2, 3)
    return (features[None], input_grad[None], weight_grad)


def solution(mesh):
    placed = (
        P("row", "col", None, None),
        P(None, None, None, "col"),
        P(),
        P("row", "col", None, None),
    )
    return jax.shard_map(
        on_device,
        mesh=mesh,
        in_specs=placed,
        out_specs=(
            P("row", "col", None, None),
            P("row", "col", None, None),
            P(None, None, None, "col"),
        ),
        check_vma=False,
    )
```

```python
import functools
import math

import jax
import jax.numpy as jnp
from jax import lax
from jax.experimental import pallas as pl
from jax.experimental.pallas import tpu as pltpu
from jax.sharding import PartitionSpec as P

epsilon = 1e-06
root_half = 0.7071067811865476
norm_const = 0.3989422804014327
MESH = pl.DeviceIdType.MESH
NT = (((1,), (1,)), ((), ()))


def norm_act(conv_out, upper, norm_gain):
    mean_val = jnp.mean(conv_out, axis=-1, keepdims=True)
    centred = conv_out - mean_val
    variance = jnp.mean(centred * centred, axis=-1, keepdims=True)
    inv_std = lax.rsqrt(variance + epsilon)
    unit = centred * inv_std
    normed = unit * norm_gain
    cdf_val = 0.5 * (1.0 + lax.erf(normed * root_half))
    density = jnp.exp(-0.5 * normed * normed) * norm_const
    outputs = (normed * cdf_val).astype(jnp.bfloat16)
    upstream = upper.astype(jnp.float32) * (cdf_val + normed * density) * norm_gain
    mean_up = jnp.mean(upstream, axis=-1, keepdims=True)
    mean_cross = jnp.mean(upstream * unit, axis=-1, keepdims=True)
    return (outputs, inv_std * (upstream - mean_up - unit * mean_cross))


def kernel(
    plan,
    x_ref,
    w_ref,
    gain_ref,
    cot_ref,
    feat_ref,
    igrad_ref,
    wg_ref,
    wt,
    x3,
    g3,
    gt,
    conv_even,
    conv_odd,
    g_pad,
    x_own,
    cot_own,
    feat_own,
    igrad_own,
    wg_own,
    x_halo,
    g_halo,
    parts,
    parts_in,
    gathered,
    z_in,
    *rest,
):
    rows, cols, quads, split, cs, rs = plan
    phases = quads.bit_length() - 1
    totals, totals_in = rest[: phases + 1], rest[phases + 1 : 2 * phases + 1]
    (in_sem, out_sem, halo_s, halo_r, wz_s, wz_r, wq_s, wq_r, sib_s, sib_r, ph_s, ph_r, z_s, z_r, ag_s, ag_r, all_s, all_r) = rest[
        2 * phases + 1 :
    ]
    tile_rows, width, chan = x_ref.shape
    out_chan = cs * cols
    taps = 3 * chan
    half_k = taps // 2
    half_w = 3 * half_k
    my_row, my_col = lax.axis_index("row"), lax.axis_index("col")
    quad, core = my_row // 2, my_row % 2
    sibling = (quad * 2 + 1 - core, my_col)
    bits, partners, partner_quads = [], [], []
    for j in range(phases):
        low, high = 1 << j, 1 << (phases - 1 - j)
        mask = low + core * (high - low)
        bit = (1 - core) * ((quad // low) % 2) + core * ((quad // high) % 2)
        other = quad + mask * (1 - 2 * bit)
        bits.append(bit)
        partner_quads.append(other)
        partners.append((other * 2 + core, my_col))
    started = []

    def send(src, dst, send_sem, recv_sem, device):
        copy = pltpu.make_async_remote_copy(
            src_ref=src,
            dst_ref=dst,
            send_sem=send_sem,
            recv_sem=recv_sem,
            device_id=device,
            device_id_type=MESH,
        )
        copy.start()
        started.append(copy)
        return copy

    def col_at(shift):
        return (my_col + cols + shift) % cols

    barrier = pltpu.get_barrier_semaphore()
    for d in range(1, rows):
        pl.semaphore_signal(
            barrier, inc=1, device_id=((my_row + d) % rows, my_col), device_id_type=MESH
        )
    for d in range(1, cols):
        pl.semaphore_signal(barrier, inc=1, device_id=(my_row, col_at(d)), device_id_type=MESH)

    own_rows = pl.ds(pl.multiple_of(my_col * cs, 16), cs)
    own_copies = []
    for t in range(9):
        own_copies.append(
            pltpu.make_async_copy(
                w_ref.at[t], wt.at[own_rows, t * chan : (t + 1) * chan], in_sem.at[t]
            )
        )
    x_copy = pltpu.make_async_copy(x_ref, x_own, in_sem.at[9])
    cot_copy = pltpu.make_async_copy(cot_ref, cot_own, in_sem.at[10])
    for copy in own_copies + [x_copy, cot_copy]:
        copy.start()
    for copy in own_copies:
        copy.wait()

    pl.semaphore_wait(barrier, rows + cols - 2)

    half_lanes = pl.ds(pl.multiple_of(core * half_w, 128), half_w)

    def piece(col, q):
        start = col * cs + (q * rs if split else 0)
        return wt.at[pl.ds(pl.multiple_of(start, 16), rs), half_lanes]

    def other_col(e):
        first = e + (cols + e - my_col) // cols
        last = cols - 1 - (e + (e + 1 + my_col) // cols)
        far = (2 * my_col) // cols
        return first + far * (last - first)

    own = piece(my_col, quad)
    wz = []
    for e in range(cols - 1):
        to = other_col(e)
        wz.append(
            pltpu.make_async_remote_copy(
                src_ref=own,
                dst_ref=own,
                send_sem=wz_s.at[to],
                recv_sem=wz_r.at[my_col],
                device_id=(my_row, to),
                device_id_type=MESH,
            )
        )
        wz[e].start()

    def arrived(e):
        col = other_col(e)
        got = piece(col, quad)
        pltpu.make_async_copy(got, got, wz_r.at[col]).wait()
        return col, got

    has_up, has_down = my_col > 0, my_col < cols - 1

    def halo_copies(first, last, into, base):
        up = pltpu.make_async_remote_copy(
            src_ref=first,
            dst_ref=into.at[1],
            send_sem=halo_s.at[base],
            recv_sem=halo_r.at[base],
            device_id=(my_row, col_at(-1)),
            device_id_type=MESH,
        )
        down = pltpu.make_async_remote_copy(
            src_ref=last,
            dst_ref=into.at[0],
            send_sem=halo_s.at[base + 1],
            recv_sem=halo_r.at[base + 1],
            device_id=(my_row, col_at(1)),
            device_id_type=MESH,
        )

        @pl.when(has_up)
        def _():
            up.start()

        @pl.when(has_down)
        def _():
            down.start()

        return up, down

    column = lax.broadcasted_iota(jnp.int32, (width, chan), 0)

    def spread(dst, row, value, flip):
        value = value.astype(jnp.float32)
        left = jnp.where(column == 0, 0.0, pltpu.roll(value, 1, 0))
        right = jnp.where(column == width - 1, 0.0, pltpu.roll(value, width - 1, 0))
        shifted = (right, value, left) if flip else (left, value, right)
        for c in range(3):
            dst[row, :, c * chan : (c + 1) * chan] = shifted[c].astype(jnp.bfloat16)

    def halo_rows(dst, into, copies, flip):
        up, down = copies

        @pl.when(has_up)
        def _():
            down.wait_recv()
            spread(dst, 0, into[0], flip)

        @pl.when(jnp.logical_not(has_up))
        def _():
            dst[0] = jnp.zeros(dst.shape[1:], dst.dtype)

        @pl.when(has_down)
        def _():
            up.wait_recv()
            spread(dst, tile_rows + 1, into[1], flip)

        @pl.when(jnp.logical_not(has_down))
        def _():
            dst[tile_rows + 1] = jnp.zeros(dst.shape[1:], dst.dtype)

    x_copies = halo_copies(x_ref.at[0], x_ref.at[tile_rows - 1], x_halo, 0)

    hops = {}

    def pass_on(e):
        col, got = arrived(e)
        for j in range(2):
            hops[e, j] = send(got, got, wq_s.at[e, j], wq_r.at[e, j], partners[j])

    def pass_again(e):
        hops[e, 0].wait_recv()
        got = piece(other_col(e), partner_quads[0])
        hops[e, 2] = send(got, got, wq_s.at[e, 2], wq_r.at[e, 2], partners[1])

    sib = []

    def to_sibling(e):
        if split:
            hops[e, 1].wait_recv()
            hops[e, 2].wait_recv()
            col = other_col(e)
        else:
            col, _ = arrived(e)
        block = wt.at[pl.ds(pl.multiple_of(col * cs, 16), cs), half_lanes]
        sib.append(send(block, block, sib_s.at[e], sib_r.at[e], sibling))

    def spread_rows(first, last):
        @pl.loop(first, last)
        def _(i):
            spread(x3, i + 1, x_own[i], False)

    x_copy.wait()
    steps = cols - 1
    cut = tile_rows // 4
    spread_rows(0, cut)
    if split:
        pass_on(0)
        spread_rows(cut, 2 * cut)
        for e in range(1, steps):
            pass_on(e)
            pass_again(e - 1)
            if e > 1:
                to_sibling(e - 2)
        pass_again(steps - 1)
        for e in range(max(steps - 2, 0), steps - 1):
            to_sibling(e)
        spread_rows(2 * cut, tile_rows)
        halo_rows(x3, x_halo, x_copies, False)
        to_sibling(steps - 1)
    else:
        spread_rows(cut, tile_rows)
        for e in range(steps):
            to_sibling(e)
        halo_rows(x3, x_halo, x_copies, False)
    for copy in sib:
        copy.wait_recv()

    gain = gain_ref[...]
    quarter = tile_rows // 4
    strip = 32

    def convolve(b, into):
        acc = None
        for a in range(3):
            term = lax.dot_general(
                x3[pl.ds(b * quarter + a, quarter)].reshape(quarter * width, taps),
                wt[:, a * taps : (a + 1) * taps],
                NT,
                preferred_element_type=jnp.float32,
            )
            acc = term if acc is None else acc + term
        into[...] = acc.reshape(quarter, width, out_chan)

    def act(b, source):
        for r in range(quarter):
            i = b * quarter + r
            for first in range(0, width, strip):
                span = slice(first, first + strip)
                outputs, grad_pre = norm_act(source[r, span], cot_own[i, span], gain)
                feat_own[i, span] = outputs
                g_pad[r, 8 + first : 8 + first + strip] = grad_pre
            value = g_pad[r, 8 : 8 + width].astype(jnp.bfloat16)
            g3[i + 1, :, 0:out_chan] = g_pad[r, 9 : 9 + width].astype(jnp.bfloat16)
            g3[i + 1, :, out_chan : 2 * out_chan] = value
            g3[i + 1, :, 2 * out_chan :] = g_pad[r, 7 : 7 + width].astype(jnp.bfloat16)
            gt[:, pl.ds(pl.multiple_of(i * width, 128), width)] = value.T

    g_pad[...] = jnp.zeros(g_pad.shape, g_pad.dtype)
    cot_copy.wait()
    convolve(0, conv_even)

    @pl.loop(0, 2)
    def _(t):
        convolve(2 * t + 1, conv_odd)
        act(2 * t, conv_even)
        convolve(jnp.minimum(2 * t + 2, 3), conv_even)
        act(2 * t + 1, conv_odd)

    feat_copy = pltpu.make_async_copy(feat_own, feat_ref, out_sem.at[0])
    feat_copy.start()

    centre = pl.ds(chan, chan)
    g_copies = halo_copies(g3.at[1, :, centre], g3.at[tile_rows, :, centre], g_halo, 2)

    def weight_part(k):
        acc = jnp.dot(
            gt[...],
            x3[k : k + tile_rows].reshape(tile_rows * width, taps),
            preferred_element_type=jnp.float32,
        ).astype(jnp.bfloat16)
        for h in range(2):
            for s in range(quads if split else 1):
                at = (s % 2) * 2 + s // 2 if split and h == 0 else s
                for c in range(cols):
                    first = c * cs + s * rs
                    parts[k, h, at, c] = acc[first : first + rs, h * half_k : (h + 1) * half_k]
        return send(
            parts.at[k, 1 - core], parts_in.at[k], ph_s.at[k, phases], ph_r.at[k, phases], sibling
        )

    def add(one, two):
        return (one.astype(jnp.float32) + two.astype(jnp.float32)).astype(jnp.bfloat16)

    def start_phase(k, j):
        size = totals_in[j].shape[1]
        source = totals[j].at[k, pl.ds((1 - bits[j]) * size, size)] if split else totals[j].at[k]
        return send(source, totals_in[j].at[k], ph_s.at[k, j], ph_r.at[k, j], partners[j])

    def after_siblings(k, copy):
        copy.wait_recv()
        totals[0][k] = add(parts[k, core], parts_in[k])
        return start_phase(k, 0)

    def after_phase(k, j, copy):
        copy.wait_recv()
        size = totals_in[j].shape[1]
        kept = totals[j][k, pl.ds(bits[j] * size, size)] if split else totals[j][k]
        totals[j + 1][k] = add(kept, totals_in[j][k])
        if j + 1 < phases:
            return start_phase(k, j + 1)
        return [
            send(
                totals[phases].at[k, 0, col_at(d)],
                z_in.at[k, d - 1],
                z_s.at[k, d - 1],
                z_r.at[k, d - 1],
                (my_row, col_at(d)),
            )
            for d in range(1, cols)
        ]

    at_quad = quad if split else 0

    def after_cols(k, copies):
        total = totals[phases][k, 0, my_col].astype(jnp.float32)
        for d, copy in enumerate(copies):
            copy.wait_recv()
            total = total + z_in[k, d].astype(jnp.float32)
        gathered[k, core, at_quad] = total.astype(jnp.bfloat16)
        if not split:
            return []
        own = gathered.at[k, core, quad]
        if k == 2:
            return [
                send(
                    own,
                    own,
                    all_s.at[d - 1],
                    all_r.at[my_row],
                    ((my_row + d) % rows, my_col),
                )
                for d in range(1, rows)
            ]
        return [
            send(
                own, own, ag_s.at[k, d], ag_r.at[k, d], (((quad + d) % quads) * 2 + core, my_col)
            )
            for d in range(1, quads)
        ]

    def after_quads(k, copies):
        if split and k == 2:
            for d in range(1, rows):
                row = (my_row + d) % rows
                got = gathered.at[k, row % 2, row // 2]
                pltpu.make_async_copy(got, got, all_r.at[row]).wait()
            return None
        for copy in copies:
            copy.wait_recv()
        own = gathered.at[k, core]
        return send(own, own, ag_s.at[k, 0], ag_r.at[k, 0], sibling)

    scale = 1.0 / math.sqrt(tile_rows * width * rows * cols)

    def finish(k, copy):
        if copy is not None:
            copy.wait_recv()
        for h in range(2):
            value = gathered[k, h].astype(jnp.float32).reshape(cs, half_k) * scale
            for lane in range(0, half_k, 128):
                tap, at = divmod(h * half_k + lane, chan)
                wg_own[3 * k + tap, :, at : at + 128] = value[:, lane : lane + 128]
        done = pltpu.make_async_copy(
            wg_own.at[3 * k : 3 * k + 3], wg_ref.at[3 * k : 3 * k + 3], out_sem.at[2 + k]
        )
        done.start()
        return done

    def input_part(b):
        acc = None
        for a in range(3):
            for c in range(3):
                first = b * quarter + 2 - a
                term = jnp.dot(
                    g3[first : first + quarter, :, c * chan : (c + 1) * chan].reshape(
                        quarter * width, out_chan
                    ),
                    wt[:, a * taps + c * chan : a * taps + (c + 1) * chan],
                    preferred_element_type=jnp.float32,
                )
                acc = term if acc is None else acc + term
        igrad_own[b * quarter : (b + 1) * quarter] = acc.astype(jnp.bfloat16).reshape(
            quarter, width, chan
        )

    flight = [None] * 3
    flight[0] = weight_part(0)
    flight[1] = weight_part(1)
    flight[0] = after_siblings(0, flight[0])
    flight[2] = weight_part(2)
    flight[1] = after_siblings(1, flight[1])
    flight[0] = after_phase(0, 0, flight[0])
    flight[2] = after_siblings(2, flight[2])
    input_part(1)
    flight[1] = after_phase(1, 0, flight[1])
    for j in range(1, phases):
        flight[0] = after_phase(0, j, flight[0])
    flight[2] = after_phase(2, 0, flight[2])
    input_part(2)
    for j in range(1, phases):
        flight[1] = after_phase(1, j, flight[1])
    flight[0] = after_cols(0, flight[0])
    for j in range(1, phases):
        flight[2] = after_phase(2, j, flight[2])
    halo_rows(g3, g_halo, g_copies, True)
    input_part(0)
    flight[1] = after_cols(1, flight[1])
    flight[0] = after_quads(0, flight[0])
    flight[2] = after_cols(2, flight[2])
    input_part(3)
    igrad_copy = pltpu.make_async_copy(igrad_own, igrad_ref, out_sem.at[1])
    igrad_copy.start()
    flight[1] = after_quads(1, flight[1])
    flight[0] = finish(0, flight[0])
    flight[1] = finish(1, flight[1])
    flight[2] = after_quads(2, flight[2])
    flight[2] = finish(2, flight[2])

    for copy in started + wz:
        copy.wait_send()
    for copy in [feat_copy, igrad_copy] + flight:
        copy.wait()
    for up, down in (x_copies, g_copies):

        @pl.when(has_up)
        def _():
            up.wait_send()

        @pl.when(has_down)
        def _():
            down.wait_send()


def on_device(images, weight, norm_gain, cotangent):
    _, tile_rows, width, chan = images.shape
    rows, cols = lax.axis_size("row"), lax.axis_size("col")
    cs = weight.shape[3]
    quads = rows // 2
    split = quads == 4 and cs % 64 == 0
    pieces = quads if split else 1
    rs = cs // pieces
    phases = quads.bit_length() - 1
    out_chan = cs * cols
    taps = 3 * chan
    half = taps // 2
    bf16 = jnp.bfloat16
    vmem = pltpu.VMEM
    dma = pltpu.SemaphoreType.DMA
    counts = [pieces >> j if split else 1 for j in range(phases + 1)]
    scratch = [
        vmem((out_chan, 3 * taps), bf16),
        vmem((tile_rows + 2, width, taps), bf16),
        vmem((tile_rows + 2, width, 3 * out_chan), bf16),
        vmem((out_chan, tile_rows * width), bf16),
        vmem((tile_rows // 4, width, out_chan), jnp.float32),
        vmem((tile_rows // 4, width, out_chan), jnp.float32),
        vmem((tile_rows // 4, width + 16, out_chan), jnp.float32),
        vmem((tile_rows, width, chan), bf16),
        vmem((tile_rows, width, out_chan), bf16),
        vmem((tile_rows, width, out_chan), bf16),
        vmem((tile_rows, width, chan), bf16),
        vmem((9, cs, chan), jnp.float32),
        vmem((2, width, chan), bf16),
        vmem((2, width, out_chan), bf16),
        vmem((3, 2, pieces, cols, rs, half), bf16),
        vmem((3, pieces, cols, rs, half), bf16),
        vmem((3, 2, pieces, rs, half), bf16),
        vmem((3, cols - 1, rs, half), bf16),
    ]
    scratch += [vmem((3, n, cols, rs, half), bf16) for n in counts]
    scratch += [vmem((3, n, cols, rs, half), bf16) for n in counts[1:]]
    scratch += [dma((11,)), dma((5,))]
    for shape in (
        (4,),
        (cols,),
        (cols - 1, 3),
        (cols - 1,),
        (3, phases + 1),
        (3, cols - 1),
        (3, quads),
        (rows,),
    ):
        scratch += [dma(shape), dma(shape)]
    in_hbm = pl.BlockSpec(memory_space=pltpu.HBM)
    in_vmem = pl.BlockSpec(memory_space=pltpu.VMEM)
    flops = 3 * 2 * tile_rows * width * 3 * taps * out_chan
    shapes = (
        jax.ShapeDtypeStruct((tile_rows, width, out_chan), bf16),
        jax.ShapeDtypeStruct((tile_rows, width, chan), bf16),
        jax.ShapeDtypeStruct((9, cs, chan), jnp.float32),
    )
    features, input_grad, wide_grad = pl.pallas_call(
        functools.partial(kernel, (rows, cols, quads, split, cs, rs)),
        out_shape=shapes,
        in_specs=[in_hbm, in_hbm, in_vmem, in_hbm],
        out_specs=(in_hbm,) * 3,
        scratch_shapes=scratch,
        cost_estimate=pl.CostEstimate(
            flops=flops, bytes_accessed=4 << 20, transcendentals=2 * tile_rows * width * out_chan
        ),
        compiler_params=pltpu.CompilerParams(
            collective_id=0, has_side_effects=True, vmem_limit_bytes=60 << 20
        ),
    )(
        images.reshape(tile_rows, width, chan),
        jnp.swapaxes(weight, 2, 3).reshape(9, cs, chan),
        norm_gain.reshape(1, out_chan),
        cotangent.reshape(tile_rows, width, out_chan),
    )
    weight_grad = jnp.swapaxes(wide_grad.reshape(3, 3, cs, chan), 2, 3)
    return (features[None], input_grad[None], weight_grad)


def solution(mesh):
    placed = (
        P("row", "col", None, None),
        P(None, None, None, "col"),
        P(),
        P("row", "col", None, None),
    )
    return jax.shard_map(
        on_device,
        mesh=mesh,
        in_specs=placed,
        out_specs=(
            P("row", "col", None, None),
            P("row", "col", None, None),
            P(None, None, None, "col"),
        ),
        check_vma=False,
    )
```

```python
import functools
import math

import jax
import jax.numpy as jnp
from jax import lax
from jax.experimental import pallas as pl
from jax.experimental.pallas import tpu as pltpu
from jax.sharding import PartitionSpec as P

epsilon = 1e-06
root_half = 0.7071067811865476
norm_const = 0.3989422804014327
MESH = pl.DeviceIdType.MESH
NT = (((1,), (1,)), ((), ()))


def norm_act(conv_out, upper, norm_gain):
    mean_val = jnp.mean(conv_out, axis=-1, keepdims=True)
    centred = conv_out - mean_val
    variance = jnp.mean(centred * centred, axis=-1, keepdims=True)
    inv_std = lax.rsqrt(variance + epsilon)
    unit = centred * inv_std
    normed = unit * norm_gain
    cdf_val = 0.5 * (1.0 + lax.erf(normed * root_half))
    density = jnp.exp(-0.5 * normed * normed) * norm_const
    outputs = (normed * cdf_val).astype(jnp.bfloat16)
    upstream = upper.astype(jnp.float32) * (cdf_val + normed * density) * norm_gain
    mean_up = jnp.mean(upstream, axis=-1, keepdims=True)
    mean_cross = jnp.mean(upstream * unit, axis=-1, keepdims=True)
    return (outputs, inv_std * (upstream - mean_up - unit * mean_cross))


def kernel(
    plan,
    x_ref,
    w_ref,
    gain_ref,
    cot_ref,
    feat_ref,
    igrad_ref,
    wg_ref,
    wt,
    x3,
    g3,
    gt,
    conv_even,
    conv_odd,
    g_pad,
    x_own,
    cot_own,
    feat_own,
    igrad_own,
    wg_own,
    x_halo,
    g_halo,
    parts,
    parts_in,
    gathered,
    z_in,
    *rest,
):
    rows, cols, quads, split, cs, rs = plan
    phases = quads.bit_length() - 1
    totals, totals_in = rest[: phases + 1], rest[phases + 1 : 2 * phases + 1]
    (in_sem, out_sem, halo_s, halo_r, wz_s, wz_r, wq_s, wq_r, sib_s, sib_r, ph_s, ph_r, z_s, z_r, ag_s, ag_r, all_s, all_r) = rest[
        2 * phases + 1 :
    ]
    tile_rows, width, chan = x_ref.shape
    out_chan = cs * cols
    taps = 3 * chan
    half_k = taps // 2
    half_w = 3 * half_k
    my_row, my_col = lax.axis_index("row"), lax.axis_index("col")
    quad, core = my_row // 2, my_row % 2
    sibling = (quad * 2 + 1 - core, my_col)
    bits, partners, partner_quads = [], [], []
    for j in range(phases):
        low, high = 1 << j, 1 << (phases - 1 - j)
        mask = low + core * (high - low)
        bit = (1 - core) * ((quad // low) % 2) + core * ((quad // high) % 2)
        other = quad + mask * (1 - 2 * bit)
        bits.append(bit)
        partner_quads.append(other)
        partners.append((other * 2 + core, my_col))
    started = []

    def send(src, dst, send_sem, recv_sem, device):
        copy = pltpu.make_async_remote_copy(
            src_ref=src,
            dst_ref=dst,
            send_sem=send_sem,
            recv_sem=recv_sem,
            device_id=device,
            device_id_type=MESH,
        )
        copy.start()
        started.append(copy)
        return copy

    def col_at(shift):
        return (my_col + cols + shift) % cols

    barrier = pltpu.get_barrier_semaphore()
    for d in range(1, rows):
        pl.semaphore_signal(
            barrier, inc=1, device_id=((my_row + d) % rows, my_col), device_id_type=MESH
        )
    for d in range(1, cols):
        pl.semaphore_signal(barrier, inc=1, device_id=(my_row, col_at(d)), device_id_type=MESH)

    own_rows = pl.ds(pl.multiple_of(my_col * cs, 16), cs)
    own_copies = []
    for t in range(9):
        own_copies.append(
            pltpu.make_async_copy(
                w_ref.at[t], wt.at[own_rows, t * chan : (t + 1) * chan], in_sem.at[t]
            )
        )
    x_copy = pltpu.make_async_copy(x_ref, x_own, in_sem.at[9])
    cot_copy = pltpu.make_async_copy(cot_ref, cot_own, in_sem.at[10])
    for copy in own_copies + [x_copy, cot_copy]:
        copy.start()
    for copy in own_copies:
        copy.wait()

    pl.semaphore_wait(barrier, rows + cols - 2)

    half_lanes = pl.ds(pl.multiple_of(core * half_w, 128), half_w)

    def piece(col, q):
        start = col * cs + (q * rs if split else 0)
        return wt.at[pl.ds(pl.multiple_of(start, 16), rs), half_lanes]

    def other_col(e):
        first = e + (cols + e - my_col) // cols
        last = cols - 1 - (e + (e + 1 + my_col) // cols)
        far = (2 * my_col) // cols
        return first + far * (last - first)

    own = piece(my_col, quad)
    wz = []
    for e in range(cols - 1):
        to = other_col(e)
        wz.append(
            pltpu.make_async_remote_copy(
                src_ref=own,
                dst_ref=own,
                send_sem=wz_s.at[to],
                recv_sem=wz_r.at[my_col],
                device_id=(my_row, to),
                device_id_type=MESH,
            )
        )
        wz[e].start()

    def arrived(e):
        col = other_col(e)
        got = piece(col, quad)
        pltpu.make_async_copy(got, got, wz_r.at[col]).wait()
        return col, got

    has_up, has_down = my_col > 0, my_col < cols - 1

    def halo_copies(first, last, into, base):
        up = pltpu.make_async_remote_copy(
            src_ref=first,
            dst_ref=into.at[1],
            send_sem=halo_s.at[base],
            recv_sem=halo_r.at[base],
            device_id=(my_row, col_at(-1)),
            device_id_type=MESH,
        )
        down = pltpu.make_async_remote_copy(
            src_ref=last,
            dst_ref=into.at[0],
            send_sem=halo_s.at[base + 1],
            recv_sem=halo_r.at[base + 1],
            device_id=(my_row, col_at(1)),
            device_id_type=MESH,
        )

        @pl.when(has_up)
        def _():
            up.start()

        @pl.when(has_down)
        def _():
            down.start()

        return up, down

    column = lax.broadcasted_iota(jnp.int32, (width, chan), 0)

    def spread(dst, row, value, flip):
        value = value.astype(jnp.float32)
        left = jnp.where(column == 0, 0.0, pltpu.roll(value, 1, 0))
        right = jnp.where(column == width - 1, 0.0, pltpu.roll(value, width - 1, 0))
        shifted = (right, value, left) if flip else (left, value, right)
        for c in range(3):
            dst[row, :, c * chan : (c + 1) * chan] = shifted[c].astype(jnp.bfloat16)

    def halo_rows(dst, into, copies, flip):
        up, down = copies

        @pl.when(has_up)
        def _():
            down.wait_recv()
            spread(dst, 0, into[0], flip)

        @pl.when(jnp.logical_not(has_up))
        def _():
            dst[0] = jnp.zeros(dst.shape[1:], dst.dtype)

        @pl.when(has_down)
        def _():
            up.wait_recv()
            spread(dst, tile_rows + 1, into[1], flip)

        @pl.when(jnp.logical_not(has_down))
        def _():
            dst[tile_rows + 1] = jnp.zeros(dst.shape[1:], dst.dtype)

    x_copies = halo_copies(x_ref.at[0], x_ref.at[tile_rows - 1], x_halo, 0)

    hops = {}

    def pass_on(e):
        col, got = arrived(e)
        for j in range(2):
            hops[e, j] = send(got, got, wq_s.at[e, j], wq_r.at[e, j], partners[j])

    def pass_again(e):
        hops[e, 0].wait_recv()
        got = piece(other_col(e), partner_quads[0])
        hops[e, 2] = send(got, got, wq_s.at[e, 2], wq_r.at[e, 2], partners[1])

    sib = []

    def to_sibling(e):
        if split:
            hops[e, 1].wait_recv()
            hops[e, 2].wait_recv()
            col = other_col(e)
        else:
            col, _ = arrived(e)
        block = wt.at[pl.ds(pl.multiple_of(col * cs, 16), cs), half_lanes]
        sib.append(send(block, block, sib_s.at[e], sib_r.at[e], sibling))

    def spread_rows(first, last):
        @pl.loop(first, last)
        def _(i):
            spread(x3, i + 1, x_own[i], False)

    x_copy.wait()
    steps = cols - 1
    cut = tile_rows // 4
    spread_rows(0, cut)
    if split:
        pass_on(0)
        spread_rows(cut, 2 * cut)
        for e in range(1, steps):
            pass_on(e)
            pass_again(e - 1)
            if e > 1:
                to_sibling(e - 2)
        pass_again(steps - 1)
        for e in range(max(steps - 2, 0), steps - 1):
            to_sibling(e)
        spread_rows(2 * cut, tile_rows)
        halo_rows(x3, x_halo, x_copies, False)
        to_sibling(steps - 1)
    else:
        spread_rows(cut, tile_rows)
        for e in range(steps):
            to_sibling(e)
        halo_rows(x3, x_halo, x_copies, False)
    for copy in sib:
        copy.wait_recv()

    gain = gain_ref[...]
    quarter = tile_rows // 4
    strip = 32

    def convolve(b, into):
        acc = None
        for a in range(3):
            term = lax.dot_general(
                x3[pl.ds(b * quarter + a, quarter)].reshape(quarter * width, taps),
                wt[:, a * taps : (a + 1) * taps],
                NT,
                preferred_element_type=jnp.float32,
            )
            acc = term if acc is None else acc + term
        into[...] = acc.reshape(quarter, width, out_chan)

    def act(b, source):
        for r in range(quarter):
            i = b * quarter + r
            for first in range(0, width, strip):
                span = slice(first, first + strip)
                outputs, grad_pre = norm_act(source[r, span], cot_own[i, span], gain)
                feat_own[i, span] = outputs
                g_pad[r, 8 + first : 8 + first + strip] = grad_pre
            value = g_pad[r, 8 : 8 + width].astype(jnp.bfloat16)
            g3[i + 1, :, 0:out_chan] = g_pad[r, 9 : 9 + width].astype(jnp.bfloat16)
            g3[i + 1, :, out_chan : 2 * out_chan] = value
            g3[i + 1, :, 2 * out_chan :] = g_pad[r, 7 : 7 + width].astype(jnp.bfloat16)
            gt[:, pl.ds(pl.multiple_of(i * width, 128), width)] = value.T

    g_pad[...] = jnp.zeros(g_pad.shape, g_pad.dtype)
    cot_copy.wait()
    convolve(0, conv_even)

    buffers = (conv_even, conv_odd)
    for b in range(4):
        if b < 3:
            convolve(b + 1, buffers[(b + 1) % 2])
        act(b, buffers[b % 2])

    feat_copy = pltpu.make_async_copy(feat_own, feat_ref, out_sem.at[0])
    feat_copy.start()

    centre = pl.ds(chan, chan)
    g_copies = halo_copies(g3.at[1, :, centre], g3.at[tile_rows, :, centre], g_halo, 2)

    def weight_part(k):
        acc = jnp.dot(
            gt[...],
            x3[k : k + tile_rows].reshape(tile_rows * width, taps),
            preferred_element_type=jnp.float32,
        ).astype(jnp.bfloat16)
        for h in range(2):
            for s in range(quads if split else 1):
                at = (s % 2) * 2 + s // 2 if split and h == 0 else s
                for c in range(cols):
                    first = c * cs + s * rs
                    parts[k, h, at, c] = acc[first : first + rs, h * half_k : (h + 1) * half_k]
        return send(
            parts.at[k, 1 - core], parts_in.at[k], ph_s.at[k, phases], ph_r.at[k, phases], sibling
        )

    def add(one, two):
        return (one.astype(jnp.float32) + two.astype(jnp.float32)).astype(jnp.bfloat16)

    def start_phase(k, j):
        size = totals_in[j].shape[1]
        source = totals[j].at[k, pl.ds((1 - bits[j]) * size, size)] if split else totals[j].at[k]
        return send(source, totals_in[j].at[k], ph_s.at[k, j], ph_r.at[k, j], partners[j])

    def after_siblings(k, copy):
        copy.wait_recv()
        totals[0][k] = add(parts[k, core], parts_in[k])
        return start_phase(k, 0)

    def after_phase(k, j, copy):
        copy.wait_recv()
        size = totals_in[j].shape[1]
        kept = totals[j][k, pl.ds(bits[j] * size, size)] if split else totals[j][k]
        totals[j + 1][k] = add(kept, totals_in[j][k])
        if j + 1 < phases:
            return start_phase(k, j + 1)
        return [
            send(
                totals[phases].at[k, 0, col_at(d)],
                z_in.at[k, d - 1],
                z_s.at[k, d - 1],
                z_r.at[k, d - 1],
                (my_row, col_at(d)),
            )
            for d in range(1, cols)
        ]

    at_quad = quad if split else 0

    def after_cols(k, copies):
        total = totals[phases][k, 0, my_col].astype(jnp.float32)
        for d, copy in enumerate(copies):
            copy.wait_recv()
            total = total + z_in[k, d].astype(jnp.float32)
        gathered[k, core, at_quad] = total.astype(jnp.bfloat16)
        if not split:
            return []
        own = gathered.at[k, core, quad]
        if k == 2:
            return [
                send(
                    own,
                    own,
                    all_s.at[d - 1],
                    all_r.at[my_row],
                    ((my_row + d) % rows, my_col),
                )
                for d in range(1, rows)
            ]
        return [
            send(
                own, own, ag_s.at[k, d], ag_r.at[k, d], (((quad + d) % quads) * 2 + core, my_col)
            )
            for d in range(1, quads)
        ]

    def after_quads(k, copies):
        if split and k == 2:
            for d in range(1, rows):
                row = (my_row + d) % rows
                got = gathered.at[k, row % 2, row // 2]
                pltpu.make_async_copy(got, got, all_r.at[row]).wait()
            return None
        for copy in copies:
            copy.wait_recv()
        own = gathered.at[k, core]
        return send(own, own, ag_s.at[k, 0], ag_r.at[k, 0], sibling)

    scale = 1.0 / math.sqrt(tile_rows * width * rows * cols)

    def finish(k, copy):
        if copy is not None:
            copy.wait_recv()
        for h in range(2):
            value = gathered[k, h].astype(jnp.float32).reshape(cs, half_k) * scale
            for lane in range(0, half_k, 128):
                tap, at = divmod(h * half_k + lane, chan)
                wg_own[3 * k + tap, :, at : at + 128] = value[:, lane : lane + 128]
        done = pltpu.make_async_copy(
            wg_own.at[3 * k : 3 * k + 3], wg_ref.at[3 * k : 3 * k + 3], out_sem.at[2 + k]
        )
        done.start()
        return done

    def input_part(b):
        acc = None
        for a in range(3):
            for c in range(3):
                first = b * quarter + 2 - a
                term = jnp.dot(
                    g3[first : first + quarter, :, c * chan : (c + 1) * chan].reshape(
                        quarter * width, out_chan
                    ),
                    wt[:, a * taps + c * chan : a * taps + (c + 1) * chan],
                    preferred_element_type=jnp.float32,
                )
                acc = term if acc is None else acc + term
        igrad_own[b * quarter : (b + 1) * quarter] = acc.astype(jnp.bfloat16).reshape(
            quarter, width, chan
        )

    flight = [None] * 3
    flight[0] = weight_part(0)
    flight[1] = weight_part(1)
    flight[0] = after_siblings(0, flight[0])
    flight[2] = weight_part(2)
    flight[1] = after_siblings(1, flight[1])
    flight[0] = after_phase(0, 0, flight[0])
    flight[2] = after_siblings(2, flight[2])
    input_part(1)
    flight[1] = after_phase(1, 0, flight[1])
    for j in range(1, phases):
        flight[0] = after_phase(0, j, flight[0])
    flight[2] = after_phase(2, 0, flight[2])
    input_part(2)
    for j in range(1, phases):
        flight[1] = after_phase(1, j, flight[1])
    flight[0] = after_cols(0, flight[0])
    for j in range(1, phases):
        flight[2] = after_phase(2, j, flight[2])
    halo_rows(g3, g_halo, g_copies, True)
    input_part(0)
    flight[1] = after_cols(1, flight[1])
    flight[0] = after_quads(0, flight[0])
    flight[2] = after_cols(2, flight[2])
    input_part(3)
    igrad_copy = pltpu.make_async_copy(igrad_own, igrad_ref, out_sem.at[1])
    igrad_copy.start()
    flight[1] = after_quads(1, flight[1])
    flight[0] = finish(0, flight[0])
    flight[1] = finish(1, flight[1])
    flight[2] = after_quads(2, flight[2])
    flight[2] = finish(2, flight[2])

    for copy in started + wz:
        copy.wait_send()
    for copy in [feat_copy, igrad_copy] + flight:
        copy.wait()
    for up, down in (x_copies, g_copies):

        @pl.when(has_up)
        def _():
            up.wait_send()

        @pl.when(has_down)
        def _():
            down.wait_send()


def on_device(images, weight, norm_gain, cotangent):
    _, tile_rows, width, chan = images.shape
    rows, cols = lax.axis_size("row"), lax.axis_size("col")
    cs = weight.shape[3]
    quads = rows // 2
    split = quads == 4 and cs % 64 == 0
    pieces = quads if split else 1
    rs = cs // pieces
    phases = quads.bit_length() - 1
    out_chan = cs * cols
    taps = 3 * chan
    half = taps // 2
    bf16 = jnp.bfloat16
    vmem = pltpu.VMEM
    dma = pltpu.SemaphoreType.DMA
    counts = [pieces >> j if split else 1 for j in range(phases + 1)]
    scratch = [
        vmem((out_chan, 3 * taps), bf16),
        vmem((tile_rows + 2, width, taps), bf16),
        vmem((tile_rows + 2, width, 3 * out_chan), bf16),
        vmem((out_chan, tile_rows * width), bf16),
        vmem((tile_rows // 4, width, out_chan), jnp.float32),
        vmem((tile_rows // 4, width, out_chan), jnp.float32),
        vmem((tile_rows // 4, width + 16, out_chan), jnp.float32),
        vmem((tile_rows, width, chan), bf16),
        vmem((tile_rows, width, out_chan), bf16),
        vmem((tile_rows, width, out_chan), bf16),
        vmem((tile_rows, width, chan), bf16),
        vmem((9, cs, chan), jnp.float32),
        vmem((2, width, chan), bf16),
        vmem((2, width, out_chan), bf16),
        vmem((3, 2, pieces, cols, rs, half), bf16),
        vmem((3, pieces, cols, rs, half), bf16),
        vmem((3, 2, pieces, rs, half), bf16),
        vmem((3, cols - 1, rs, half), bf16),
    ]
    scratch += [vmem((3, n, cols, rs, half), bf16) for n in counts]
    scratch += [vmem((3, n, cols, rs, half), bf16) for n in counts[1:]]
    scratch += [dma((11,)), dma((5,))]
    for shape in (
        (4,),
        (cols,),
        (cols - 1, 3),
        (cols - 1,),
        (3, phases + 1),
        (3, cols - 1),
        (3, quads),
        (rows,),
    ):
        scratch += [dma(shape), dma(shape)]
    in_hbm = pl.BlockSpec(memory_space=pltpu.HBM)
    in_vmem = pl.BlockSpec(memory_space=pltpu.VMEM)
    flops = 3 * 2 * tile_rows * width * 3 * taps * out_chan
    shapes = (
        jax.ShapeDtypeStruct((tile_rows, width, out_chan), bf16),
        jax.ShapeDtypeStruct((tile_rows, width, chan), bf16),
        jax.ShapeDtypeStruct((9, cs, chan), jnp.float32),
    )
    features, input_grad, wide_grad = pl.pallas_call(
        functools.partial(kernel, (rows, cols, quads, split, cs, rs)),
        out_shape=shapes,
        in_specs=[in_hbm, in_hbm, in_vmem, in_hbm],
        out_specs=(in_hbm,) * 3,
        scratch_shapes=scratch,
        cost_estimate=pl.CostEstimate(
            flops=flops, bytes_accessed=4 << 20, transcendentals=2 * tile_rows * width * out_chan
        ),
        compiler_params=pltpu.CompilerParams(
            collective_id=0, has_side_effects=True, vmem_limit_bytes=60 << 20
        ),
    )(
        images.reshape(tile_rows, width, chan),
        jnp.swapaxes(weight, 2, 3).reshape(9, cs, chan),
        norm_gain.reshape(1, out_chan),
        cotangent.reshape(tile_rows, width, out_chan),
    )
    weight_grad = jnp.swapaxes(wide_grad.reshape(3, 3, cs, chan), 2, 3)
    return (features[None], input_grad[None], weight_grad)


def solution(mesh):
    placed = (
        P("row", "col", None, None),
        P(None, None, None, "col"),
        P(),
        P("row", "col", None, None),
    )
    return jax.shard_map(
        on_device,
        mesh=mesh,
        in_specs=placed,
        out_specs=(
            P("row", "col", None, None),
            P("row", "col", None, None),
            P(None, None, None, "col"),
        ),
        check_vma=False,
    )
```

```python
import functools
import math

import jax
import jax.numpy as jnp
from jax import lax
from jax.experimental import pallas as pl
from jax.experimental.pallas import tpu as pltpu
from jax.sharding import PartitionSpec as P

epsilon = 1e-06
root_half = 0.7071067811865476
norm_const = 0.3989422804014327
MESH = pl.DeviceIdType.MESH
NT = (((1,), (1,)), ((), ()))


def norm_act(conv_out, upper, norm_gain):
    mean_val = jnp.mean(conv_out, axis=-1, keepdims=True)
    centred = conv_out - mean_val
    variance = jnp.mean(centred * centred, axis=-1, keepdims=True)
    inv_std = lax.rsqrt(variance + epsilon)
    unit = centred * inv_std
    normed = unit * norm_gain
    cdf_val = 0.5 * (1.0 + lax.erf(normed * root_half))
    density = jnp.exp(-0.5 * normed * normed) * norm_const
    outputs = (normed * cdf_val).astype(jnp.bfloat16)
    upstream = upper.astype(jnp.float32) * (cdf_val + normed * density) * norm_gain
    mean_up = jnp.mean(upstream, axis=-1, keepdims=True)
    mean_cross = jnp.mean(upstream * unit, axis=-1, keepdims=True)
    return (outputs, inv_std * (upstream - mean_up - unit * mean_cross))


def kernel(
    plan,
    x_ref,
    w_ref,
    gain_ref,
    cot_ref,
    feat_ref,
    igrad_ref,
    wg_ref,
    wt,
    x3,
    g3,
    gt,
    conv_even,
    conv_odd,
    g_pad,
    x_own,
    cot_own,
    feat_own,
    igrad_own,
    wg_own,
    x_halo,
    g_halo,
    parts,
    parts_in,
    gathered,
    z_in,
    *rest,
):
    rows, cols, quads, split, cs, rs = plan
    phases = quads.bit_length() - 1
    totals, totals_in = rest[: phases + 1], rest[phases + 1 : 2 * phases + 1]
    (in_sem, out_sem, halo_s, halo_r, wz_s, wz_r, wq_s, wq_r, sib_s, sib_r, ph_s, ph_r, z_s, z_r, ag_s, ag_r, all_s, all_r) = rest[
        2 * phases + 1 :
    ]
    tile_rows, width, chan = x_ref.shape
    out_chan = cs * cols
    taps = 3 * chan
    half_k = taps // 2
    half_w = 3 * half_k
    my_row, my_col = lax.axis_index("row"), lax.axis_index("col")
    quad, core = my_row // 2, my_row % 2
    sibling = (quad * 2 + 1 - core, my_col)
    bits, partners, partner_quads = [], [], []
    for j in range(phases):
        low, high = 1 << j, 1 << (phases - 1 - j)
        mask = low + core * (high - low)
        bit = (1 - core) * ((quad // low) % 2) + core * ((quad // high) % 2)
        other = quad + mask * (1 - 2 * bit)
        bits.append(bit)
        partner_quads.append(other)
        partners.append((other * 2 + core, my_col))
    started = []

    def send(src, dst, send_sem, recv_sem, device):
        copy = pltpu.make_async_remote_copy(
            src_ref=src,
            dst_ref=dst,
            send_sem=send_sem,
            recv_sem=recv_sem,
            device_id=device,
            device_id_type=MESH,
        )
        copy.start()
        started.append(copy)
        return copy

    def col_at(shift):
        return (my_col + cols + shift) % cols

    barrier = pltpu.get_barrier_semaphore()
    for d in range(1, rows):
        pl.semaphore_signal(
            barrier, inc=1, device_id=((my_row + d) % rows, my_col), device_id_type=MESH
        )
    for d in range(1, cols):
        pl.semaphore_signal(barrier, inc=1, device_id=(my_row, col_at(d)), device_id_type=MESH)

    own_rows = pl.ds(pl.multiple_of(my_col * cs, 16), cs)
    own_copies = []
    for t in range(9):
        own_copies.append(
            pltpu.make_async_copy(
                w_ref.at[t], wt.at[own_rows, t * chan : (t + 1) * chan], in_sem.at[t]
            )
        )
    x_copy = pltpu.make_async_copy(x_ref, x_own, in_sem.at[9])
    cot_copy = pltpu.make_async_copy(cot_ref, cot_own, in_sem.at[10])
    for copy in own_copies + [x_copy, cot_copy]:
        copy.start()
    for copy in own_copies:
        copy.wait()

    pl.semaphore_wait(barrier, rows + cols - 2)

    half_lanes = pl.ds(pl.multiple_of(core * half_w, 128), half_w)

    def piece(col, q):
        start = col * cs + (q * rs if split else 0)
        return wt.at[pl.ds(pl.multiple_of(start, 16), rs), half_lanes]

    def other_col(e):
        first = e + (cols + e - my_col) // cols
        last = cols - 1 - (e + (e + 1 + my_col) // cols)
        far = (2 * my_col) // cols
        return first + far * (last - first)

    own = piece(my_col, quad)
    wz = []
    for e in range(cols - 1):
        to = other_col(e)
        wz.append(
            pltpu.make_async_remote_copy(
                src_ref=own,
                dst_ref=own,
                send_sem=wz_s.at[to],
                recv_sem=wz_r.at[my_col],
                device_id=(my_row, to),
                device_id_type=MESH,
            )
        )
        wz[e].start()

    def arrived(e):
        col = other_col(e)
        got = piece(col, quad)
        pltpu.make_async_copy(got, got, wz_r.at[col]).wait()
        return col, got

    has_up, has_down = my_col > 0, my_col < cols - 1

    def halo_copies(first, last, into, base):
        up = pltpu.make_async_remote_copy(
            src_ref=first,
            dst_ref=into.at[1],
            send_sem=halo_s.at[base],
            recv_sem=halo_r.at[base],
            device_id=(my_row, col_at(-1)),
            device_id_type=MESH,
        )
        down = pltpu.make_async_remote_copy(
            src_ref=last,
            dst_ref=into.at[0],
            send_sem=halo_s.at[base + 1],
            recv_sem=halo_r.at[base + 1],
            device_id=(my_row, col_at(1)),
            device_id_type=MESH,
        )

        @pl.when(has_up)
        def _():
            up.start()

        @pl.when(has_down)
        def _():
            down.start()

        return up, down

    column = lax.broadcasted_iota(jnp.int32, (width, chan), 0)

    def spread(dst, row, value, flip):
        value = value.astype(jnp.float32)
        left = jnp.where(column == 0, 0.0, pltpu.roll(value, 1, 0))
        right = jnp.where(column == width - 1, 0.0, pltpu.roll(value, width - 1, 0))
        shifted = (right, value, left) if flip else (left, value, right)
        for c in range(3):
            dst[row, :, c * chan : (c + 1) * chan] = shifted[c].astype(jnp.bfloat16)

    def halo_rows(dst, into, copies, flip):
        up, down = copies

        @pl.when(has_up)
        def _():
            down.wait_recv()
            spread(dst, 0, into[0], flip)

        @pl.when(jnp.logical_not(has_up))
        def _():
            dst[0] = jnp.zeros(dst.shape[1:], dst.dtype)

        @pl.when(has_down)
        def _():
            up.wait_recv()
            spread(dst, tile_rows + 1, into[1], flip)

        @pl.when(jnp.logical_not(has_down))
        def _():
            dst[tile_rows + 1] = jnp.zeros(dst.shape[1:], dst.dtype)

    x_copies = halo_copies(x_ref.at[0], x_ref.at[tile_rows - 1], x_halo, 0)

    hops = {}

    def pass_on(e):
        col, got = arrived(e)
        for j in range(2):
            hops[e, j] = send(got, got, wq_s.at[e, j], wq_r.at[e, j], partners[j])

    def pass_again(e):
        hops[e, 0].wait_recv()
        got = piece(other_col(e), partner_quads[0])
        hops[e, 2] = send(got, got, wq_s.at[e, 2], wq_r.at[e, 2], partners[1])

    sib = []

    def to_sibling(e):
        if split:
            hops[e, 1].wait_recv()
            hops[e, 2].wait_recv()
            col = other_col(e)
        else:
            col, _ = arrived(e)
        block = wt.at[pl.ds(pl.multiple_of(col * cs, 16), cs), half_lanes]
        sib.append(send(block, block, sib_s.at[e], sib_r.at[e], sibling))

    def spread_rows(first, last):
        @pl.loop(first, last)
        def _(i):
            spread(x3, i + 1, x_own[i], False)

    x_copy.wait()
    steps = cols - 1
    cut = tile_rows // 4
    spread_rows(0, cut)
    if split:
        pass_on(0)
        spread_rows(cut, 2 * cut)
        for e in range(1, steps):
            pass_on(e)
            pass_again(e - 1)
            if e > 1:
                to_sibling(e - 2)
        pass_again(steps - 1)
        for e in range(max(steps - 2, 0), steps - 1):
            to_sibling(e)
        spread_rows(2 * cut, tile_rows)
        halo_rows(x3, x_halo, x_copies, False)
        to_sibling(steps - 1)
    else:
        spread_rows(cut, tile_rows)
        for e in range(steps):
            to_sibling(e)
        halo_rows(x3, x_halo, x_copies, False)
    for copy in sib:
        copy.wait_recv()

    gain = gain_ref[...]
    quarter = tile_rows // 4
    strip = 64

    def convolve(b, into):
        acc = None
        for a in range(3):
            term = lax.dot_general(
                x3[pl.ds(b * quarter + a, quarter)].reshape(quarter * width, taps),
                wt[:, a * taps : (a + 1) * taps],
                NT,
                preferred_element_type=jnp.float32,
            )
            acc = term if acc is None else acc + term
        into[...] = acc.reshape(quarter, width, out_chan)

    def act(b, source):
        for r in range(quarter):
            i = b * quarter + r
            for first in range(0, width, strip):
                span = slice(first, first + strip)
                outputs, grad_pre = norm_act(source[r, span], cot_own[i, span], gain)
                feat_own[i, span] = outputs
                g_pad[r, 8 + first : 8 + first + strip] = grad_pre
            value = g_pad[r, 8 : 8 + width].astype(jnp.bfloat16)
            g3[i + 1, :, 0:out_chan] = g_pad[r, 9 : 9 + width].astype(jnp.bfloat16)
            g3[i + 1, :, out_chan : 2 * out_chan] = value
            g3[i + 1, :, 2 * out_chan :] = g_pad[r, 7 : 7 + width].astype(jnp.bfloat16)
            gt[:, pl.ds(pl.multiple_of(i * width, 128), width)] = value.T

    g_pad[...] = jnp.zeros(g_pad.shape, g_pad.dtype)
    cot_copy.wait()
    convolve(0, conv_even)

    buffers = (conv_even, conv_odd)
    for b in range(4):
        if b < 3:
            convolve(b + 1, buffers[(b + 1) % 2])
        act(b, buffers[b % 2])

    feat_copy = pltpu.make_async_copy(feat_own, feat_ref, out_sem.at[0])
    feat_copy.start()

    centre = pl.ds(chan, chan)
    g_copies = halo_copies(g3.at[1, :, centre], g3.at[tile_rows, :, centre], g_halo, 2)

    def weight_part(k):
        acc = jnp.dot(
            gt[...],
            x3[k : k + tile_rows].reshape(tile_rows * width, taps),
            preferred_element_type=jnp.float32,
        ).astype(jnp.bfloat16)
        for h in range(2):
            for s in range(quads if split else 1):
                at = (s % 2) * 2 + s // 2 if split and h == 0 else s
                for c in range(cols):
                    first = c * cs + s * rs
                    parts[k, h, at, c] = acc[first : first + rs, h * half_k : (h + 1) * half_k]
        return send(
            parts.at[k, 1 - core], parts_in.at[k], ph_s.at[k, phases], ph_r.at[k, phases], sibling
        )

    def add(one, two):
        return (one.astype(jnp.float32) + two.astype(jnp.float32)).astype(jnp.bfloat16)

    def start_phase(k, j):
        size = totals_in[j].shape[1]
        source = totals[j].at[k, pl.ds((1 - bits[j]) * size, size)] if split else totals[j].at[k]
        return send(source, totals_in[j].at[k], ph_s.at[k, j], ph_r.at[k, j], partners[j])

    def after_siblings(k, copy):
        copy.wait_recv()
        totals[0][k] = add(parts[k, core], parts_in[k])
        return start_phase(k, 0)

    def after_phase(k, j, copy):
        copy.wait_recv()
        size = totals_in[j].shape[1]
        kept = totals[j][k, pl.ds(bits[j] * size, size)] if split else totals[j][k]
        totals[j + 1][k] = add(kept, totals_in[j][k])
        if j + 1 < phases:
            return start_phase(k, j + 1)
        return [
            send(
                totals[phases].at[k, 0, col_at(d)],
                z_in.at[k, d - 1],
                z_s.at[k, d - 1],
                z_r.at[k, d - 1],
                (my_row, col_at(d)),
            )
            for d in range(1, cols)
        ]

    at_quad = quad if split else 0

    def after_cols(k, copies):
        total = totals[phases][k, 0, my_col].astype(jnp.float32)
        for d, copy in enumerate(copies):
            copy.wait_recv()
            total = total + z_in[k, d].astype(jnp.float32)
        gathered[k, core, at_quad] = total.astype(jnp.bfloat16)
        if not split:
            return []
        own = gathered.at[k, core, quad]
        if k == 2:
            return [
                send(
                    own,
                    own,
                    all_s.at[d - 1],
                    all_r.at[my_row],
                    ((my_row + d) % rows, my_col),
                )
                for d in range(1, rows)
            ]
        return [
            send(
                own, own, ag_s.at[k, d], ag_r.at[k, d], (((quad + d) % quads) * 2 + core, my_col)
            )
            for d in range(1, quads)
        ]

    def after_quads(k, copies):
        if split and k == 2:
            for d in range(1, rows):
                row = (my_row + d) % rows
                got = gathered.at[k, row % 2, row // 2]
                pltpu.make_async_copy(got, got, all_r.at[row]).wait()
            return None
        for copy in copies:
            copy.wait_recv()
        own = gathered.at[k, core]
        return send(own, own, ag_s.at[k, 0], ag_r.at[k, 0], sibling)

    scale = 1.0 / math.sqrt(tile_rows * width * rows * cols)

    def finish(k, copy):
        if copy is not None:
            copy.wait_recv()
        for h in range(2):
            value = gathered[k, h].astype(jnp.float32).reshape(cs, half_k) * scale
            for lane in range(0, half_k, 128):
                tap, at = divmod(h * half_k + lane, chan)
                wg_own[3 * k + tap, :, at : at + 128] = value[:, lane : lane + 128]
        done = pltpu.make_async_copy(
            wg_own.at[3 * k : 3 * k + 3], wg_ref.at[3 * k : 3 * k + 3], out_sem.at[2 + k]
        )
        done.start()
        return done

    def input_part(b):
        acc = None
        for a in range(3):
            for c in range(3):
                first = b * quarter + 2 - a
                term = jnp.dot(
                    g3[first : first + quarter, :, c * chan : (c + 1) * chan].reshape(
                        quarter * width, out_chan
                    ),
                    wt[:, a * taps + c * chan : a * taps + (c + 1) * chan],
                    preferred_element_type=jnp.float32,
                )
                acc = term if acc is None else acc + term
        igrad_own[b * quarter : (b + 1) * quarter] = acc.astype(jnp.bfloat16).reshape(
            quarter, width, chan
        )

    flight = [None] * 3
    flight[0] = weight_part(0)
    flight[1] = weight_part(1)
    flight[0] = after_siblings(0, flight[0])
    flight[2] = weight_part(2)
    flight[1] = after_siblings(1, flight[1])
    flight[0] = after_phase(0, 0, flight[0])
    flight[2] = after_siblings(2, flight[2])
    input_part(1)
    flight[1] = after_phase(1, 0, flight[1])
    for j in range(1, phases):
        flight[0] = after_phase(0, j, flight[0])
    flight[2] = after_phase(2, 0, flight[2])
    input_part(2)
    for j in range(1, phases):
        flight[1] = after_phase(1, j, flight[1])
    flight[0] = after_cols(0, flight[0])
    for j in range(1, phases):
        flight[2] = after_phase(2, j, flight[2])
    halo_rows(g3, g_halo, g_copies, True)
    input_part(0)
    flight[1] = after_cols(1, flight[1])
    flight[0] = after_quads(0, flight[0])
    flight[2] = after_cols(2, flight[2])
    input_part(3)
    igrad_copy = pltpu.make_async_copy(igrad_own, igrad_ref, out_sem.at[1])
    igrad_copy.start()
    flight[1] = after_quads(1, flight[1])
    flight[0] = finish(0, flight[0])
    flight[1] = finish(1, flight[1])
    flight[2] = after_quads(2, flight[2])
    flight[2] = finish(2, flight[2])

    for copy in started + wz:
        copy.wait_send()
    for copy in [feat_copy, igrad_copy] + flight:
        copy.wait()
    for up, down in (x_copies, g_copies):

        @pl.when(has_up)
        def _():
            up.wait_send()

        @pl.when(has_down)
        def _():
            down.wait_send()


def on_device(images, weight, norm_gain, cotangent):
    _, tile_rows, width, chan = images.shape
    rows, cols = lax.axis_size("row"), lax.axis_size("col")
    cs = weight.shape[3]
    quads = rows // 2
    split = quads == 4 and cs % 64 == 0
    pieces = quads if split else 1
    rs = cs // pieces
    phases = quads.bit_length() - 1
    out_chan = cs * cols
    taps = 3 * chan
    half = taps // 2
    bf16 = jnp.bfloat16
    vmem = pltpu.VMEM
    dma = pltpu.SemaphoreType.DMA
    counts = [pieces >> j if split else 1 for j in range(phases + 1)]
    scratch = [
        vmem((out_chan, 3 * taps), bf16),
        vmem((tile_rows + 2, width, taps), bf16),
        vmem((tile_rows + 2, width, 3 * out_chan), bf16),
        vmem((out_chan, tile_rows * width), bf16),
        vmem((tile_rows // 4, width, out_chan), jnp.float32),
        vmem((tile_rows // 4, width, out_chan), jnp.float32),
        vmem((tile_rows // 4, width + 16, out_chan), jnp.float32),
        vmem((tile_rows, width, chan), bf16),
        vmem((tile_rows, width, out_chan), bf16),
        vmem((tile_rows, width, out_chan), bf16),
        vmem((tile_rows, width, chan), bf16),
        vmem((9, cs, chan), jnp.float32),
        vmem((2, width, chan), bf16),
        vmem((2, width, out_chan), bf16),
        vmem((3, 2, pieces, cols, rs, half), bf16),
        vmem((3, pieces, cols, rs, half), bf16),
        vmem((3, 2, pieces, rs, half), bf16),
        vmem((3, cols - 1, rs, half), bf16),
    ]
    scratch += [vmem((3, n, cols, rs, half), bf16) for n in counts]
    scratch += [vmem((3, n, cols, rs, half), bf16) for n in counts[1:]]
    scratch += [dma((11,)), dma((5,))]
    for shape in (
        (4,),
        (cols,),
        (cols - 1, 3),
        (cols - 1,),
        (3, phases + 1),
        (3, cols - 1),
        (3, quads),
        (rows,),
    ):
        scratch += [dma(shape), dma(shape)]
    in_hbm = pl.BlockSpec(memory_space=pltpu.HBM)
    in_vmem = pl.BlockSpec(memory_space=pltpu.VMEM)
    flops = 3 * 2 * tile_rows * width * 3 * taps * out_chan
    shapes = (
        jax.ShapeDtypeStruct((tile_rows, width, out_chan), bf16),
        jax.ShapeDtypeStruct((tile_rows, width, chan), bf16),
        jax.ShapeDtypeStruct((9, cs, chan), jnp.float32),
    )
    features, input_grad, wide_grad = pl.pallas_call(
        functools.partial(kernel, (rows, cols, quads, split, cs, rs)),
        out_shape=shapes,
        in_specs=[in_hbm, in_hbm, in_vmem, in_hbm],
        out_specs=(in_hbm,) * 3,
        scratch_shapes=scratch,
        cost_estimate=pl.CostEstimate(
            flops=flops, bytes_accessed=4 << 20, transcendentals=2 * tile_rows * width * out_chan
        ),
        compiler_params=pltpu.CompilerParams(
            collective_id=0, has_side_effects=True, vmem_limit_bytes=60 << 20
        ),
    )(
        images.reshape(tile_rows, width, chan),
        jnp.swapaxes(weight, 2, 3).reshape(9, cs, chan),
        norm_gain.reshape(1, out_chan),
        cotangent.reshape(tile_rows, width, out_chan),
    )
    weight_grad = jnp.swapaxes(wide_grad.reshape(3, 3, cs, chan), 2, 3)
    return (features[None], input_grad[None], weight_grad)


def solution(mesh):
    placed = (
        P("row", "col", None, None),
        P(None, None, None, "col"),
        P(),
        P("row", "col", None, None),
    )
    return jax.shard_map(
        on_device,
        mesh=mesh,
        in_specs=placed,
        out_specs=(
            P("row", "col", None, None),
            P("row", "col", None, None),
            P(None, None, None, "col"),
        ),
        check_vma=False,
    )
```
